512 devices in a mesh: section: 8 (over z), cp: 16 (over x, y_lo), tp: 4 (over y_hi, core).
Axes of the slice: x: 4, y: 8 (y_hi: 2, y_lo: 4; y = y_hi * 4 + y_lo), z: 8, core: 2. Of those that a mesh axis runs over, the one named last changes fastest.
Arguments:
- queries: bfloat16 [2, 8, 512, 4096], P(None, 'section', 'cp', 'tp'), may hold values from -90 to 90
- key_rows: bfloat16 [8, 24576, 512], P('section', 'cp', 'tp'), may hold values from -13 to 13
- value_rows: bfloat16 [8, 24576, 512], P('section', 'cp', 'tp'), may hold values from -8 to 8
- section_rows: bfloat16 [8, 512, 4096], P('section', 'cp', 'tp'), may hold values from -60 to 60
- fresh_rows: bfloat16 [512, 4096], P('cp', 'tp'), may hold values from -60 to 60
- norm_gain: bfloat16 [8, 4096], P('section', 'tp'), may hold values from 0.25 to 1.75
- segment_lengths: int32 [9], replicated, may hold values from 256 to 512, as said below
Outputs:
- residual: bfloat16 [2, 8, 512, 4096], P(None, 'section', 'cp', 'tp')
- normed: bfloat16 [2, 8, 512, 4096], P(None, 'section', 'cp', 'tp')
The draws below stay inside these ranges and needn't reach their ends.
Inputs may be any that keep to these rules, and one draw needn't show every extreme that they name: `segment_lengths`: every segment has 256 to 512 live rows and some segment has all 512.
All inputs are finite; a program needn't handle non-finite values.
Results may differ from the reference program's by a relative error of at most 0.008.
Values may be sent and summed in bfloat16 or wider, within the bound.
No kernel may reach another device: no remote copies, remote signals or barrier semaphores. Data moves between devices by JAX's collectives and lax.ppermute only.
A program may use at most 64 MiB of HBM per device.

```python
import jax
import jax.numpy as jnp
from jax import lax

HD = 128
HEADS = 32
KV_HEADS = 4
WIDTH = 4096
KV_WIDTH = 512
SEGMENT = 512
CTX = 24576
N_SECTION = 8


def key_base(base_key):
    noise = jax.random.normal(base_key, (N_SECTION, CTX, KV_HEADS, HD), jnp.float32)
    return 1.75 * jnp.clip(noise, -6.0, 6.0)


def scaled_rows(row_key, noise, ramp):
    shape = noise.shape
    row_scale = 10.0 ** (jax.random.uniform(row_key, shape[:-1], jnp.float32) - 0.5)
    column_ids = jnp.arange(shape[-1], dtype=jnp.float32) / shape[-1]
    column_scale = ramp ** column_ids / jnp.sqrt(ramp)
    return noise * row_scale[..., None] * column_scale


def draw_key_rows(key, part):
    base = key_base(key)
    return base.reshape(N_SECTION, CTX, KV_HEADS * HD).astype(jnp.bfloat16)


def draw_queries(key, part):
    key = jax.random.fold_in(key, 5)
    drawn_key = jax.random.fold_in(key, 0)
    shape = (2, N_SECTION, SEGMENT, HEADS, HD)
    drawn = 1.75 * jnp.clip(jax.random.normal(drawn_key, shape, jnp.float32), -6.0, 6.0)
    return drawn.reshape(2, N_SECTION, SEGMENT, HEADS * HD).astype(jnp.bfloat16)


def draw_section_rows(key, part):
    key = jax.random.fold_in(key, 7)
    noise_key, row_key = jax.random.split(key, 2)
    shape = (N_SECTION, SEGMENT, HEADS * HD)
    noise = jnp.clip(jax.random.normal(noise_key, shape, jnp.float32), -6.0, 6.0)
    ramp = 3.0
    return scaled_rows(row_key, noise, ramp).astype(jnp.bfloat16)


def draw_fresh_rows(key, part):
    key = jax.random.fold_in(key, 9)
    noise_key, row_key = jax.random.split(key, 2)
    shape = (SEGMENT, HEADS * HD)
    noise = jnp.clip(jax.random.normal(noise_key, shape, jnp.float32), -6.0, 6.0)
    ramp = 3.0
    return scaled_rows(row_key, noise, ramp).astype(jnp.bfloat16)


def draw_segment_lengths(key, part):
    key = jax.random.fold_in(key, 13)
    length_key, full_key = jax.random.split(key, 2)
    lengths = jax.random.randint(length_key, (N_SECTION + 1,), SEGMENT // 2, SEGMENT + 1)
    full_one = jax.random.randint(full_key, (), 0, N_SECTION + 1)
    return jnp.where(jnp.arange(N_SECTION + 1) == full_one, SEGMENT, lengths).astype(jnp.int32)


def block_levels(rng, shape, cuts, least, top_value):
    def one(axis_at, blocks):
        draws = jax.random.uniform(jax.random.fold_in(jax.random.fold_in(rng, 6), axis_at), (blocks,), jnp.float32, least / len(cuts), top_value / len(cuts))
        return jnp.repeat(jnp.exp(draws), shape[axis_at] // blocks).reshape((-1,) + (1,) * (len(shape) - axis_at - 1))

    factor_of = one(*cuts[0])
    for cut in cuts[1:]:
        factor_of = factor_of * one(*cut)
    return factor_of


def normal_values(stream_key, extent, scale, bound, cuts=(), kind=jnp.bfloat16):
    values = jax.random.normal(stream_key, extent, jnp.float32) * scale
    if len(cuts) > 0:
        values = block_levels(stream_key, extent, cuts, -0.22, 0.18) * values
    return jnp.clip(values, min=-bound, max=bound).astype(kind)


def setup_inputs(seed: int = 0) -> dict:
    key_list = jax.random.split(jax.random.key(seed), 8)
    queries = draw_queries(jax.random.fold_in(key_list[7], 71), 0)
    key_rows = draw_key_rows(jax.random.fold_in(key_list[7], 71), 0)
    value_rows = normal_values(key_list[2], (N_SECTION, CTX, KV_WIDTH), 2.0, 8.0, ((0, 8), (1, 16), (2, 4)))
    section_rows = draw_section_rows(jax.random.fold_in(key_list[7], 71), 0)
    fresh_rows = draw_fresh_rows(jax.random.fold_in(key_list[7], 71), 0)
    norm_gain = jnp.clip(1.0 + 0.15 * jax.random.normal(key_list[5], (N_SECTION, WIDTH), jnp.float32), 0.25, 1.75).astype(jnp.bfloat16)
    segment_lengths = draw_segment_lengths(jax.random.fold_in(key_list[7], 71), 0)
    return dict(queries=queries, key_rows=key_rows, value_rows=value_rows, section_rows=section_rows, fresh_rows=fresh_rows, norm_gain=norm_gain, segment_lengths=segment_lengths)


NEGATIVE = -1e+30
EPSILON = 1e-05

def one_head(query_head, key_head, value_head, query_pos, live_rows):
    score_scale = HD ** (-0.5)
    scores = jnp.dot(query_head, key_head.T, preferred_element_type=jnp.float32) * score_scale
    key_pos = jnp.arange(CTX, dtype=jnp.int32)
    visible = key_pos[None, :] <= query_pos[:, None]
    row_top = lax.optimization_barrier(jnp.max(jnp.where(visible, scores, NEGATIVE), axis=1, keepdims=True))
    weights = jnp.where(visible, jnp.exp(scores - row_top), 0.0)
    totals = lax.optimization_barrier(jnp.sum(weights, axis=1, keepdims=True))
    mixed = jnp.dot(weights.astype(jnp.bfloat16), value_head, preferred_element_type=jnp.float32)
    return jnp.where(live_rows[:, None], mixed / totals, 0.0)

def attend_section(query_rows, section_keys, section_values, start, length):
    group_size = HEADS // KV_HEADS
    row_ids = jnp.arange(SEGMENT, dtype=jnp.int32)
    query_pos = (start + row_ids).astype(jnp.int32)
    live_rows = row_ids < length
    query_heads = query_rows.reshape(SEGMENT, HEADS, HD).transpose(1, 0, 2)
    key_heads = section_keys.reshape(CTX, KV_HEADS, HD).transpose(1, 0, 2)
    value_heads = section_values.reshape(CTX, KV_HEADS, HD).transpose(1, 0, 2)

    def per_head(head_id):
        return one_head(query_heads[head_id], key_heads[head_id // group_size], value_heads[head_id // group_size], query_pos, live_rows)
    mixed = lax.map(per_head, jnp.arange(HEADS, dtype=jnp.int32))
    return mixed.transpose(1, 0, 2).reshape(SEGMENT, WIDTH)

def finish(row_sums, gain):
    mean_square = lax.optimization_barrier(jnp.mean(row_sums * row_sums, axis=-1, keepdims=True))
    return (row_sums * lax.rsqrt(mean_square + EPSILON) * gain.astype(jnp.float32)).astype(jnp.bfloat16)

def reference(queries, key_rows, value_rows, section_rows, fresh_rows, norm_gain, segment_lengths):
    lengths = segment_lengths.astype(jnp.int32)
    prefix = (CTX - jnp.sum(lengths)).astype(jnp.int32)
    starts = (prefix + jnp.cumsum(lengths) - lengths).astype(jnp.int32)
    residual_one, normed_one, residual_two, normed_two = ([], [], [], [])
    for section_id in range(N_SECTION):
        first_seg = N_SECTION - 1 - section_id
        attended = attend_section(queries[0, section_id], key_rows[section_id], value_rows[section_id], starts[first_seg], lengths[first_seg])
        row_sums = section_rows[section_id].astype(jnp.float32) + attended
        residual_one.append(row_sums.astype(jnp.bfloat16))
        normed_one.append(finish(row_sums, norm_gain[section_id]))
    for section_id in range(N_SECTION):
        second_seg = N_SECTION - section_id
        incoming = fresh_rows if section_id == 0 else residual_one[section_id - 1]
        attended = attend_section(queries[1, section_id], key_rows[section_id], value_rows[section_id], starts[second_seg], lengths[second_seg])
        row_sums = incoming.astype(jnp.float32) + attended
        residual_two.append(row_sums.astype(jnp.bfloat16))
        normed_two.append(finish(row_sums, norm_gain[section_id]))
    residual = jnp.stack([jnp.stack(residual_one), jnp.stack(residual_two)])
    normed = jnp.stack([jnp.stack(normed_one), jnp.stack(normed_two)])
    return (residual, normed)
```

```python
import functools

import jax
import jax.numpy as jnp
import numpy as np
from jax import lax
from jax.experimental import pallas as pl
from jax.experimental.pallas import tpu as pltpu
from jax.sharding import Mesh
from jax.sharding import PartitionSpec as P

HD = 128
NX, NY = 4, 4
HEADS_DEV = 8
ROWS = 32
WIDTH_DEV = HEADS_DEV * HD
KEYS = 1536
CTX = KEYS * NX * NY
N_SEG = 9
FULL_WIDTH = 4096
PACKED = WIDTH_DEV + 128
TILE = 512
NEGATIVE = -1e30
EPSILON = 1e-05
LOG2_SCALE = float(np.log2(np.e) / np.sqrt(HD))
VMEM_LIMIT = 56 * 2**20


def segment_of(tick):
    return 7 - lax.axis_index("section") + tick


def segment_start(lengths_ref, segment):
    start = jnp.int32(CTX)
    for j in range(N_SEG):
        start = start - jnp.where(j >= segment, lengths_ref[j], 0)
    return start


def attend_kernel(tick, lengths_ref, q_ref, k_ref, v_ref, o_ref):
    cx = lax.axis_index("cx")
    cy = lax.axis_index("cy")
    start = segment_start(lengths_ref, segment_of(tick))
    q = jnp.concatenate(
        [q_ref[j, :, h * HD : (h + 1) * HD] for j in range(NY) for h in range(HEADS_DEV)], 0
    )
    rows = q.shape[0]
    row_id = lax.broadcasted_iota(jnp.int32, (rows, 1), 0)
    per_owner = HEADS_DEV * ROWS
    in_segment = (cx * NY + row_id // per_owner) * ROWS + row_id % ROWS
    last_offset = start + in_segment - ((NX - 1) * NY + cy) * KEYS

    top = out = total = None
    for c in range(NX):
        for t in range(KEYS // TILE):
            kt = k_ref[c, t * TILE : (t + 1) * TILE, :]
            vt = v_ref[c, t * TILE : (t + 1) * TILE, :]
            s = lax.dot_general(q, kt, (((1,), (1,)), ((), ())), preferred_element_type=jnp.float32)
            if c == NX - 1:
                offset = t * TILE + lax.broadcasted_iota(jnp.int32, (1, TILE), 1)
                s = jnp.where(offset <= last_offset, s, NEGATIVE)
            part = s[:, :HD]
            for u in range(1, TILE // HD):
                part = jnp.maximum(part, s[:, u * HD : (u + 1) * HD])
            tile_top = jnp.max(part, axis=1, keepdims=True) * LOG2_SCALE
            new_top = tile_top if top is None else jnp.maximum(top, tile_top)
            p = jnp.exp2(s * LOG2_SCALE - new_top)
            lane_sum = p[:, :HD]
            for u in range(1, TILE // HD):
                lane_sum = lane_sum + p[:, u * HD : (u + 1) * HD]
            mixed = jnp.dot(p.astype(jnp.bfloat16), vt, preferred_element_type=jnp.float32)
            if top is None:
                out, total = mixed, lane_sum
            else:
                rescale = jnp.exp2(top - new_top)
                out = out * rescale + mixed
                total = total * rescale + lane_sum
            top = new_top
    total = jnp.sum(total, axis=1, keepdims=True)
    out = (out / total).astype(jnp.bfloat16)
    level = top + jnp.log2(total)

    lane = lax.broadcasted_iota(jnp.int32, (ROWS, 128), 1)
    for j in range(NY):
        packed = jnp.zeros((ROWS, 128), jnp.float32)
        for h in range(HEADS_DEV):
            at = (j * HEADS_DEV + h) * ROWS
            o_ref[j, :, h * HD : (h + 1) * HD] = out[at : at + ROWS]
            packed = jnp.where(lane % HEADS_DEV == h, level[at : at + ROWS], packed)
        high = packed.astype(jnp.bfloat16).astype(jnp.float32)
        middle = (packed - high).astype(jnp.bfloat16).astype(jnp.float32)
        low = packed - high - middle
        pieces = jnp.where(
            lane < HEADS_DEV,
            high,
            jnp.where(lane < 2 * HEADS_DEV, middle, jnp.where(lane < 3 * HEADS_DEV, low, 0.0)),
        )
        o_ref[j, :, WIDTH_DEV:] = pieces.astype(jnp.bfloat16)


def attend(tick, lengths, q_all, k_all, v_all):
    return pl.pallas_call(
        functools.partial(attend_kernel, tick),
        grid=(1,),
        in_specs=[
            pl.BlockSpec(memory_space=pltpu.SMEM),
            pl.BlockSpec((NY, None, ROWS, WIDTH_DEV), lambda i: (0, tick, 0, 0)),
            pl.BlockSpec((NX, KEYS, HD), lambda i: (0, 0, 0)),
            pl.BlockSpec((NX, KEYS, HD), lambda i: (0, 0, 0)),
        ],
        out_specs=pl.BlockSpec((NY, ROWS, PACKED), lambda i: (0, 0, 0)),
        out_shape=jax.ShapeDtypeStruct((NY, ROWS, PACKED), jnp.bfloat16),
        compiler_params=pltpu.CompilerParams(vmem_limit_bytes=VMEM_LIMIT),
        name=f"attend_{tick}",
    )(lengths, q_all, k_all, v_all)


def merged(parts_ref, live):
    levels = []
    for y in range(NY):
        pieces = parts_ref[y, :, WIDTH_DEV:].astype(jnp.float32)
        levels.append(
            pieces[:, :HEADS_DEV]
            + pieces[:, HEADS_DEV : 2 * HEADS_DEV]
            + pieces[:, 2 * HEADS_DEV : 3 * HEADS_DEV]
        )
    top = functools.reduce(jnp.maximum, levels)
    shares = [jnp.exp2(level - top) for level in levels]
    inverse = 1.0 / functools.reduce(jnp.add, shares)
    shares = [share * inverse for share in shares]
    columns = []
    for h in range(HEADS_DEV):
        total = jnp.zeros((ROWS, HD), jnp.float32)
        for y in range(NY):
            part = parts_ref[y, :, h * HD : (h + 1) * HD].astype(jnp.float32)
            total = total + shares[y][:, h : h + 1] * part
        columns.append(total)
    return jnp.where(live, jnp.concatenate(columns, 1), 0.0)


def live_rows(lengths_ref, tick):
    first = (lax.axis_index("cx") * NY + lax.axis_index("cy")) * ROWS
    row = first + lax.broadcasted_iota(jnp.int32, (ROWS, 1), 0)
    return row < lengths_ref[segment_of(tick)]


def merge_one_kernel(lengths_ref, parts_ref, rows_ref, residual_ref, sum_ref):
    total = rows_ref[...].astype(jnp.float32) + merged(parts_ref, live_rows(lengths_ref, 0))
    sum_ref[...] = total
    residual_ref[...] = total.astype(jnp.bfloat16)


def merge_two_kernel(
    lengths_ref, parts_ref, passed_ref, fresh_ref, one_ref, sum_one_ref, residual_ref, sum_ref, squares_ref
):
    first = lax.axis_index("section") == 0
    incoming = jnp.where(first, fresh_ref[...].astype(jnp.float32), passed_ref[...].astype(jnp.float32))
    total = incoming + merged(parts_ref, live_rows(lengths_ref, 1))
    sum_ref[...] = total
    residual_ref[0] = one_ref[...]
    residual_ref[1] = total.astype(jnp.bfloat16)
    sum_one = sum_one_ref[...]
    lane = lax.broadcasted_iota(jnp.int32, (ROWS, 128), 1)
    squares_ref[...] = jnp.where(
        lane < 64,
        jnp.sum(sum_one * sum_one, axis=1, keepdims=True),
        jnp.sum(total * total, axis=1, keepdims=True),
    )


def norm_kernel(squares_ref, sum_one_ref, sum_two_ref, gain_ref, normed_ref):
    scale = lax.rsqrt(squares_ref[...] / FULL_WIDTH + EPSILON)
    gain = gain_ref[...].astype(jnp.float32)
    normed_ref[0] = (sum_one_ref[...] * scale[:, 0:1] * gain).astype(jnp.bfloat16)
    normed_ref[1] = (sum_two_ref[...] * scale[:, 64:65] * gain).astype(jnp.bfloat16)


SMEM = pl.BlockSpec(memory_space=pltpu.SMEM)
VMEM = pl.BlockSpec(memory_space=pltpu.VMEM)


def shaped(shape, dtype):
    return jax.ShapeDtypeStruct(shape, dtype)


def body(queries, key_rows, value_rows, section_rows, fresh_rows, norm_gain, segment_lengths):
    q_own = jnp.broadcast_to(queries[:, 0], (NY, 2, ROWS, WIDTH_DEV))
    q_all = lax.all_to_all(q_own, "cy", 0, 0)
    k_all = lax.all_gather(key_rows[0], "cx")
    v_all = lax.all_gather(value_rows[0], "cx")

    parts_one = lax.all_to_all(attend(0, segment_lengths, q_all, k_all, v_all), "cy", 0, 0)
    parts_two = lax.all_to_all(attend(1, segment_lengths, q_all, k_all, v_all), "cy", 0, 0)

    rows_f32 = shaped((ROWS, WIDTH_DEV), jnp.float32)
    residual_one, sum_one = pl.pallas_call(
        merge_one_kernel,
        in_specs=[SMEM, VMEM, VMEM],
        out_specs=[VMEM, VMEM],
        out_shape=[shaped((ROWS, WIDTH_DEV), jnp.bfloat16), rows_f32],
        name="merge_one",
    )(segment_lengths, parts_one, section_rows[0])
    count = lax.axis_size("section")
    passed = lax.ppermute(residual_one, "section", [(i, i + 1) for i in range(count - 1)])
    residual, sum_two, squares = pl.pallas_call(
        merge_two_kernel,
        in_specs=[SMEM] + [VMEM] * 5,
        out_specs=[VMEM, VMEM, VMEM],
        out_shape=[
            shaped((2, ROWS, WIDTH_DEV), jnp.bfloat16),
            rows_f32,
            shaped((ROWS, 128), jnp.float32),
        ],
        name="merge_two",
    )(segment_lengths, parts_two, passed, fresh_rows, residual_one, sum_one)
    squares = lax.psum(squares, "tp")
    normed = pl.pallas_call(
        norm_kernel,
        in_specs=[VMEM] * 4,
        out_specs=VMEM,
        out_shape=shaped((2, ROWS, WIDTH_DEV), jnp.bfloat16),
        name="norm",
    )(squares, sum_one, sum_two, norm_gain)
    return residual[:, None], normed[:, None]


def solution(mesh):
    grid = Mesh(mesh.devices.reshape(8, NX, NY, 4), ("section", "cx", "cy", "tp"))
    cp = ("cx", "cy")
    in_specs = (
        P(None, "section", cp, "tp"),
        P("section", cp, "tp"),
        P("section", cp, "tp"),
        P("section", cp, "tp"),
        P(cp, "tp"),
        P("section", "tp"),
        P(),
    )
    out_specs = (P(None, "section", cp, "tp"), P(None, "section", cp, "tp"))
    return jax.shard_map(body, mesh=grid, in_specs=in_specs, out_specs=out_specs, check_vma=False)
```

```python
import functools

import jax
import jax.numpy as jnp
import numpy as np
from jax import lax
from jax.experimental import pallas as pl
from jax.experimental.pallas import tpu as pltpu
from jax.sharding import Mesh
from jax.sharding import PartitionSpec as P

HD = 128
NX, NY = 4, 4
HEADS_DEV = 8
ROWS = 32
WIDTH_DEV = HEADS_DEV * HD
KEYS = 1536
CTX = KEYS * NX * NY
N_SEG = 9
FULL_WIDTH = 4096
PACKED = 2 * WIDTH_DEV + 128
TILE = 512
NEGATIVE = -1e30
FLOOR = -1e28
TINY = 1e-30
EPSILON = 1e-05
LOG2_SCALE = float(np.log2(np.e) / np.sqrt(HD))
VMEM_LIMIT = 16 * 2**20
SMALL = pltpu.CompilerParams(vmem_limit_bytes=4 * 2**20)


def segment_of(tick):
    return 7 - lax.axis_index("section") + tick


def segment_start(lengths_ref, segment):
    start = jnp.int32(CTX)
    for j in range(N_SEG):
        start = start - jnp.where(j >= segment, lengths_ref[j], 0)
    return start


def init_state(rows):
    return jnp.zeros((rows, HD), jnp.float32), jnp.full((rows, HD), FLOOR, jnp.float32)


def update(state, started, q, k_tiles, v_tiles, last_offset):
    out, top = state
    lane = lax.broadcasted_iota(jnp.int32, out.shape, 1)
    total = jnp.where(lane == 0, 1.0, 0.0) if started else jnp.zeros(out.shape, jnp.float32)
    for t in range(KEYS // TILE):
        s = lax.dot_general(
            q, k_tiles(t), (((1,), (1,)), ((), ())), preferred_element_type=jnp.float32
        )
        if last_offset is not None:
            offset = t * TILE + lax.broadcasted_iota(jnp.int32, (1, TILE), 1)
            s = jnp.where(offset <= last_offset, s, NEGATIVE)
        part = s[:, :HD]
        for u in range(1, TILE // HD):
            part = jnp.maximum(part, s[:, u * HD : (u + 1) * HD])
        tile_top = jnp.max(part, axis=1, keepdims=True) * LOG2_SCALE
        new_top = jnp.maximum(top, jnp.broadcast_to(tile_top, top.shape))
        groups = [
            jnp.exp2(s[:, u * HD : (u + 1) * HD] * LOG2_SCALE - new_top)
            for u in range(TILE // HD)
        ]
        lane_sum = functools.reduce(jnp.add, groups)
        p = jnp.concatenate([group.astype(jnp.bfloat16) for group in groups], 1)
        mixed = jnp.dot(p, v_tiles(t), preferred_element_type=jnp.float32)
        rescale = jnp.exp2(top - new_top)
        out = out * rescale + mixed
        total = total * rescale + lane_sum
        top = new_top
    total = jnp.maximum(jnp.sum(total, axis=1, keepdims=True), TINY)
    return out * (1.0 / total), top + jnp.log2(total)


def write_packed(state, tick, outs):
    out, level = state
    out = out.astype(jnp.bfloat16)
    lane = lax.broadcasted_iota(jnp.int32, (ROWS, 128), 1)
    head = lane % HEADS_DEV
    piece = lane % (3 * HEADS_DEV) // HEADS_DEV
    for d, o_ref in enumerate(outs):
        levels = jnp.zeros((ROWS, 128), jnp.float32)
        for h in range(HEADS_DEV):
            at = (d * HEADS_DEV + h) * ROWS
            column = pl.multiple_of(tick * WIDTH_DEV + h * HD, HD)
            o_ref[:, pl.ds(column, HD)] = out[at : at + ROWS]
            levels = jnp.where(head == h, level[at : at + ROWS], levels)
        high = levels.astype(jnp.bfloat16).astype(jnp.float32)
        middle = (levels - high).astype(jnp.bfloat16).astype(jnp.float32)
        low = levels - high - middle
        pieces = jnp.where(piece == 0, high, jnp.where(piece == 1, middle, low))
        kept = jnp.where(tick == 0, 0.0, o_ref[:, 2 * WIDTH_DEV :].astype(jnp.float32))
        mine = lane // (3 * HEADS_DEV) == tick
        o_ref[:, 2 * WIDTH_DEV :] = jnp.where(mine, pieces, kept).astype(jnp.bfloat16)


def chunk_kernel(shift, first, last, *refs):
    lengths_ref, q_ref, kv_ref = refs[:3]
    state_in, outs = ([], refs[3:]) if first else (refs[3:5], refs[5:])
    cx = lax.axis_index("cx")
    cy = lax.axis_index("cy")
    key_start = ((cx + shift) % NX * NY + cy) * KEYS

    def one(tick):
        start = segment_start(lengths_ref, segment_of(tick))
        least = start + cx * NY * ROWS - key_start
        full = least >= KEYS - 1
        none = least + NY * ROWS - 1 < 0
        rows = NY * HEADS_DEV * ROWS

        def load():
            return init_state(rows) if first else tuple(ref[tick] for ref in state_in)

        def store(state):
            if last:
                write_packed(state, tick, outs)
            else:
                for ref, value in zip(outs, state, strict=True):
                    ref[tick] = value

        def run(masked):
            q = jnp.concatenate(
                [
                    q_ref[cy ^ d, tick, :, h * HD : (h + 1) * HD]
                    for d in range(NY)
                    for h in range(HEADS_DEV)
                ],
                0,
            )
            last_offset = None
            if masked:
                row_id = lax.broadcasted_iota(jnp.int32, (rows, 1), 0)
                owner = (row_id // (HEADS_DEV * ROWS)) ^ cy
                last_offset = least + owner * ROWS + row_id % ROWS
            store(
                update(
                    load(),
                    not first,
                    q,
                    lambda t: kv_ref[0, t * TILE : (t + 1) * TILE, :],
                    lambda t: kv_ref[1, t * TILE : (t + 1) * TILE, :],
                    last_offset,
                )
            )

        @pl.when(full)
        def _():
            run(False)

        @pl.when(jnp.logical_not(jnp.logical_or(full, none)))
        def _():
            run(True)

        @pl.when(none)
        def _():
            store(load())

    lax.fori_loop(0, 2, lambda tick, _: one(tick), None)


def stage_kernel(k_ref, v_ref, q_ref, kv_ref, q_own_ref, q_held, sems):
    q_copy = pltpu.make_async_copy(q_ref, q_held, sems.at[0])
    copies = [
        pltpu.make_async_copy(k_ref, kv_ref.at[0], sems.at[1]),
        pltpu.make_async_copy(v_ref, kv_ref.at[1], sems.at[2]),
    ]
    q_copy.start()
    for copy in copies:
        copy.start()
    q_copy.wait()
    for y in range(NY):
        copies.append(pltpu.make_async_copy(q_held, q_own_ref.at[y], sems.at[3 + y]))
        copies[-1].start()
    for copy in copies:
        copy.wait()


def in_vmem(x):
    return pltpu.with_memory_space_constraint(x, pltpu.VMEM)


def in_hbm(x):
    return pltpu.with_memory_space_constraint(x, pltpu.HBM)


def attend_chunk(lengths, q_all, kv, state, shift, last=False):
    first = state is None
    rows = NY * HEADS_DEV * ROWS
    if last:
        out_shape = [pltpu.VMEM((ROWS, PACKED), jnp.bfloat16)] * NY
    else:
        out_shape = [pltpu.VMEM((2, rows, HD), jnp.float32)] * 2
    operands = [q_all, kv] + ([] if first else list(state))
    return pl.pallas_call(
        functools.partial(chunk_kernel, shift, first, last),
        in_specs=[SMEM] + [VMEM] * len(operands),
        out_specs=[VMEM] * len(out_shape),
        out_shape=out_shape,
        compiler_params=pltpu.CompilerParams(vmem_limit_bytes=VMEM_LIMIT),
        name=f"attend_{shift}",
    )(lengths, *[in_vmem(x) for x in operands])


def merged(parts, tick, live):
    levels = []
    for part_ref in parts:
        pieces = part_ref[:, 2 * WIDTH_DEV :].astype(jnp.float32)
        levels.append(
            pieces
            + pltpu.roll(pieces, 128 - HEADS_DEV, 1)
            + pltpu.roll(pieces, 128 - 2 * HEADS_DEV, 1)
        )
    top = functools.reduce(jnp.maximum, levels)
    shares = [jnp.exp2(level - top) for level in levels]
    inverse = 1.0 / functools.reduce(jnp.add, shares)
    shares = [share * inverse for share in shares]
    columns = []
    for h in range(HEADS_DEV):
        total = jnp.zeros((ROWS, HD), jnp.float32)
        column = tick * WIDTH_DEV + h * HD
        lane = tick * 3 * HEADS_DEV + h
        for part_ref, share in zip(parts, shares, strict=True):
            part = part_ref[:, column : column + HD].astype(jnp.float32)
            total = total + share[:, lane : lane + 1] * part
        columns.append(total)
    return jnp.where(live, jnp.concatenate(columns, 1), 0.0)


def live_rows(lengths_ref, tick):
    first = (lax.axis_index("cx") * NY + lax.axis_index("cy")) * ROWS
    row = first + lax.broadcasted_iota(jnp.int32, (ROWS, 1), 0)
    return row < lengths_ref[segment_of(tick)]


def merge_kernel(lengths_ref, rows_ref, *refs):
    parts, (residual_ref, sum_ref, attended_ref) = refs[:NY], refs[NY:]
    total = rows_ref[...].astype(jnp.float32) + merged(parts, 0, live_rows(lengths_ref, 0))
    sum_ref[...] = total
    residual_ref[...] = total.astype(jnp.bfloat16)
    attended_ref[...] = merged(parts, 1, live_rows(lengths_ref, 1))


def add_kernel(
    attended_ref, passed_ref, fresh_ref, one_ref, sum_one_ref, residual_ref, sum_ref, squares_ref
):
    first = lax.axis_index("section") == 0
    incoming = jnp.where(first, fresh_ref[...].astype(jnp.float32), passed_ref[...].astype(jnp.float32))
    total = incoming + attended_ref[...]
    sum_ref[...] = total
    residual_ref[0] = one_ref[...]
    residual_ref[1] = total.astype(jnp.bfloat16)
    ones = jnp.ones((8, WIDTH_DEV), jnp.float32)
    for tick, rows in enumerate((sum_one_ref[...], total)):
        squares = lax.dot_general(
            ones,
            rows * rows,
            (((1,), (1,)), ((), ())),
            precision=lax.Precision.HIGHEST,
            preferred_element_type=jnp.float32,
        )
        squares_ref[tick : tick + 1, :] = squares[:1]


def norm_kernel(squares_ref, sum_one_ref, sum_two_ref, gain_ref, normed_ref):
    gain = gain_ref[...].astype(jnp.float32)
    row = lax.broadcasted_iota(jnp.int32, (ROWS, ROWS), 0)
    lane = lax.broadcasted_iota(jnp.int32, (ROWS, ROWS), 1)
    for tick, sum_ref in enumerate((sum_one_ref, sum_two_ref)):
        scale = lax.rsqrt(squares_ref[tick : tick + 1, :] / FULL_WIDTH + EPSILON)
        column = jnp.sum(jnp.where(row == lane, scale, 0.0), axis=1, keepdims=True)
        normed_ref[tick] = (sum_ref[...] * column * gain).astype(jnp.bfloat16)


SMEM = pl.BlockSpec(memory_space=pltpu.SMEM)
VMEM = pl.BlockSpec(memory_space=pltpu.VMEM)


def shaped(shape, dtype):
    return jax.ShapeDtypeStruct(shape, dtype)


def body(queries, key_rows, value_rows, section_rows, fresh_rows, norm_gain, segment_lengths):
    def along_x(value, by):
        return lax.ppermute(value, "cx", [(i, (i + by) % NX) for i in range(NX)])

    kv, q_own = pl.pallas_call(
        stage_kernel,
        in_specs=[pl.BlockSpec(memory_space=pl.ANY)] * 3,
        out_specs=[VMEM, pl.BlockSpec(memory_space=pl.ANY)],
        out_shape=[
            pltpu.VMEM((2, KEYS, HD), jnp.bfloat16),
            jax.ShapeDtypeStruct((NY, 2, ROWS, WIDTH_DEV), jnp.bfloat16),
        ],
        scratch_shapes=[
            pltpu.VMEM((2, ROWS, WIDTH_DEV), jnp.bfloat16),
            pltpu.SemaphoreType.DMA((3 + NY,)),
        ],
        compiler_params=SMALL,
        name="stage",
    )(*[in_hbm(x) for x in (key_rows[0], value_rows[0], queries[:, 0])])
    below = along_x(kv, 1)
    above = along_x(kv, -1)
    q_all = lax.all_to_all(q_own, "cy", 0, 0)
    below, q_all = lax.optimization_barrier((below, q_all))
    far = along_x(below, 1)

    state = attend_chunk(segment_lengths, q_all, kv, None, 0)
    state = attend_chunk(segment_lengths, q_all, below, state, NX - 1)
    state = attend_chunk(segment_lengths, q_all, above, state, 1)
    packed = attend_chunk(segment_lengths, q_all, far, state, 2, last=True)
    parts = [packed[0]] + [None] * (NY - 1)
    for d in (3, 2, 1):
        parts[d] = lax.ppermute(packed[d], "cy", [(i, i ^ d) for i in range(NY)])

    rows_bf16 = pltpu.VMEM((ROWS, WIDTH_DEV), jnp.bfloat16)
    rows_f32 = pltpu.VMEM((ROWS, WIDTH_DEV), jnp.float32)
    residual_one, sum_one, attended_two = pl.pallas_call(
        merge_kernel,
        in_specs=[SMEM] + [VMEM] * (1 + NY),
        out_specs=[VMEM] * 3,
        out_shape=[rows_bf16, rows_f32, rows_f32],
        compiler_params=SMALL,
        name="merge",
    )(segment_lengths, in_vmem(section_rows[0]), *[in_vmem(x) for x in parts])
    count = lax.axis_size("section")
    passed = lax.ppermute(residual_one, "section", [(i, i + 1) for i in range(count - 1)])
    residual, sum_two, squares = pl.pallas_call(
        add_kernel,
        in_specs=[VMEM] * 5,
        out_specs=[VMEM] * 3,
        out_shape=[
            jax.ShapeDtypeStruct((2, ROWS, WIDTH_DEV), jnp.bfloat16),
            rows_f32,
            pltpu.VMEM((2, ROWS), jnp.float32),
        ],
        compiler_params=SMALL,
        name="add",
    )(*[in_vmem(x) for x in (attended_two, passed, fresh_rows, residual_one, sum_one)])
    squares = lax.psum(squares, "tp")
    normed = pl.pallas_call(
        norm_kernel,
        in_specs=[VMEM] * 4,
        out_specs=VMEM,
        out_shape=jax.ShapeDtypeStruct((2, ROWS, WIDTH_DEV), jnp.bfloat16),
        compiler_params=SMALL,
        name="norm",
    )(in_vmem(squares), in_vmem(sum_one), in_vmem(sum_two), in_vmem(norm_gain))
    return residual[:, None], normed[:, None]


def solution(mesh):
    grid = Mesh(mesh.devices.reshape(8, NX, NY, 4), ("section", "cx", "cy", "tp"))
    cp = ("cx", "cy")
    in_specs = (
        P(None, "section", cp, "tp"),
        P("section", cp, "tp"),
        P("section", cp, "tp"),
        P("section", cp, "tp"),
        P(cp, "tp"),
        P("section", "tp"),
        P(),
    )
    out_specs = (P(None, "section", cp, "tp"), P(None, "section", cp, "tp"))
    return jax.shard_map(body, mesh=grid, in_specs=in_specs, out_specs=out_specs, check_vma=False)
```

```python
import functools

import jax
import jax.numpy as jnp
import numpy as np
from jax import lax
from jax.experimental import pallas as pl
from jax.experimental.pallas import tpu as pltpu
from jax.sharding import Mesh
from jax.sharding import PartitionSpec as P

HD = 128
NX, NY = 4, 4
HEADS_DEV = 8
ROWS = 32
WIDTH_DEV = HEADS_DEV * HD
KEYS = 1536
CTX = KEYS * NX * NY
N_SEG = 9
FULL_WIDTH = 4096
PACKED = 2 * WIDTH_DEV + 128
TILE = 1536
BLOCK = 2 * HEADS_DEV * ROWS
HALF = 2 * BLOCK
NEGATIVE = -1e30
FLOOR = -1e28
TINY = 1e-30
EPSILON = 1e-05
LOG2_SCALE = float(np.log2(np.e) / np.sqrt(HD))
VMEM_LIMIT = 24 * 2**20
LARGE = pltpu.CompilerParams(vmem_limit_bytes=VMEM_LIMIT)
SMALL = pltpu.CompilerParams(vmem_limit_bytes=4 * 2**20)


SMEM = pl.BlockSpec(memory_space=pltpu.SMEM)
VMEM = pl.BlockSpec(memory_space=pltpu.VMEM)
ANY = pl.BlockSpec(memory_space=pl.ANY)


def segment_of(tick):
    return 7 - lax.axis_index("section") + tick


def segment_start(lengths_ref, segment):
    start = jnp.int32(CTX)
    for j in range(N_SEG):
        start = start - jnp.where(j >= segment, lengths_ref[j], 0)
    return start


def update(q, k_ref, v_ref, last_offset, out_ref, top_ref, total_ref):
    def one(t, _):
        tile = pl.ds(pl.multiple_of(t * TILE, TILE), TILE)
        s = lax.dot_general(
            q, k_ref[tile], (((1,), (1,)), ((), ())), preferred_element_type=jnp.float32
        )
        if last_offset is not None:
            offset = t * TILE + lax.broadcasted_iota(jnp.int32, (1, TILE), 1)
            s = jnp.where(offset <= last_offset, s, NEGATIVE)
        part = s[:, :HD]
        for u in range(1, TILE // HD):
            part = jnp.maximum(part, s[:, u * HD : (u + 1) * HD])
        top = top_ref[...]
        tile_top = jnp.max(part, axis=1, keepdims=True) * LOG2_SCALE
        new_top = jnp.maximum(top, jnp.broadcast_to(tile_top, top.shape))
        groups = [
            jnp.exp2(s[:, u * HD : (u + 1) * HD] * LOG2_SCALE - new_top)
            for u in range(TILE // HD)
        ]
        lane_sum = functools.reduce(jnp.add, groups)
        p = jnp.concatenate([group.astype(jnp.bfloat16) for group in groups], 1)
        mixed = jnp.dot(p, v_ref[tile], preferred_element_type=jnp.float32)
        rescale = jnp.exp2(top - new_top)
        out_ref[...] = out_ref[...] * rescale + mixed
        total_ref[...] = total_ref[...] * rescale + lane_sum
        top_ref[...] = new_top

    lax.fori_loop(0, KEYS // TILE, one, None)


def finished(out_ref, top_ref, total_ref):
    total = jnp.maximum(jnp.sum(total_ref[...], axis=1, keepdims=True), TINY)
    return out_ref[...] * (1.0 / total), top_ref[...] + jnp.log2(total)


def write_packed(state, outs):
    out, level = state
    out = out.astype(jnp.bfloat16)
    lane = lax.broadcasted_iota(jnp.int32, (ROWS, 128), 1)
    head = lane % HEADS_DEV
    piece = lane % (3 * HEADS_DEV) // HEADS_DEV
    for i, o_ref in enumerate(outs):
        levels = jnp.zeros((ROWS, 128), jnp.float32)
        for tick in range(2):
            mine = lane // (3 * HEADS_DEV) == tick
            for h in range(HEADS_DEV):
                at = ((i * 2 + tick) * HEADS_DEV + h) * ROWS
                column = tick * WIDTH_DEV + h * HD
                o_ref[:, column : column + HD] = out[at : at + ROWS]
                levels = jnp.where(jnp.logical_and(mine, head == h), level[at : at + ROWS], levels)
        high = levels.astype(jnp.bfloat16).astype(jnp.float32)
        middle = (levels - high).astype(jnp.bfloat16).astype(jnp.float32)
        low = levels - high - middle
        pieces = jnp.where(piece == 0, high, jnp.where(piece == 1, middle, low))
        o_ref[:, 2 * WIDTH_DEV :] = pieces.astype(jnp.bfloat16)


def attend_rows(first_d, n_d, shift, lengths_ref, q_ref, k_ref, v_ref, state):
    cx = lax.axis_index("cx")
    cy = lax.axis_index("cy")
    base = cx * NY * ROWS - ((cx + shift) % NX * NY + cy) * KEYS
    least = [segment_start(lengths_ref, segment_of(tick)) + base for tick in range(2)]
    full = jnp.minimum(least[0], least[1]) >= KEYS - 1
    none = jnp.maximum(least[0], least[1]) + NY * ROWS - 1 < 0

    def run(masked):
        q = jnp.concatenate(
            [
                q_ref[cy ^ (first_d + i), tick, :, h * HD : (h + 1) * HD]
                for i in range(n_d)
                for tick in range(2)
                for h in range(HEADS_DEV)
            ],
            0,
        )
        last_offset = None
        if masked:
            row_id = lax.broadcasted_iota(jnp.int32, (n_d * BLOCK, 1), 0)
            owner = (first_d + row_id // BLOCK) ^ cy
            second = row_id // (BLOCK // 2) % 2 == 1
            last_offset = jnp.where(second, least[1], least[0]) + owner * ROWS + row_id % ROWS
        update(q, k_ref, v_ref, last_offset, *state)

    @pl.when(full)
    def _():
        run(False)

    @pl.when(jnp.logical_not(jnp.logical_or(full, none)))
    def _():
        run(True)


def first_kernel(lengths_ref, q_ref, k_ref, v_ref, out_ref, top_ref, total_ref):
    out_ref[...] = jnp.zeros(out_ref.shape, jnp.float32)
    top_ref[...] = jnp.full(top_ref.shape, FLOOR, jnp.float32)
    total_ref[...] = jnp.zeros(total_ref.shape, jnp.float32)

    def one(half, _):
        state = [ref.at[half] for ref in (out_ref, top_ref, total_ref)]
        attend_rows(2 * half, 2, 0, lengths_ref, q_ref, k_ref, v_ref, state)

    lax.fori_loop(0, 2, one, None)


def second_kernel(lengths_ref, q_ref, k_ref, v_ref, *refs):
    inputs, outs = refs[:3], refs[3:]

    def one(half, _):
        for source, target in zip(inputs, outs, strict=True):
            target[half] = source[half]
        state = [ref.at[half] for ref in outs]
        attend_rows(2 * half, 2, NX - 1, lengths_ref, q_ref, k_ref, v_ref, state)

    lax.fori_loop(0, 2, one, None)


def last_kernel(first_d, n_d, *refs):
    lengths_ref, q_ref, k_above, v_above, k_far, v_far = refs[:6]
    inputs, outs, state = refs[6:9], refs[9 : 9 + n_d], refs[9 + n_d :]
    begin = first_d % 2 * BLOCK
    for source, target in zip(inputs, state, strict=True):
        target[...] = source[first_d // 2, begin : begin + n_d * BLOCK]
    attend_rows(first_d, n_d, 1, lengths_ref, q_ref, k_above, v_above, state)
    attend_rows(first_d, n_d, 2, lengths_ref, q_ref, k_far, v_far, state)
    write_packed(finished(*state), outs)


def in_vmem(x):
    return pltpu.with_memory_space_constraint(x, pltpu.VMEM)


def in_hbm(x):
    return pltpu.with_memory_space_constraint(x, pltpu.HBM)


def attend_first(lengths, q_all, k, v):
    return pl.pallas_call(
        first_kernel,
        in_specs=[SMEM] + [VMEM] * 3,
        out_specs=[VMEM] * 3,
        out_shape=[pltpu.VMEM((2, HALF, HD), jnp.float32)] * 3,
        compiler_params=LARGE,
        name="attend_own",
    )(lengths, in_vmem(q_all), in_vmem(k), in_vmem(v))


def attend_second(lengths, *operands):
    return pl.pallas_call(
        second_kernel,
        in_specs=[SMEM] + [VMEM] * len(operands),
        out_specs=[VMEM] * 3,
        out_shape=[pltpu.VMEM((2, HALF, HD), jnp.float32)] * 3,
        compiler_params=LARGE,
        name="attend_below",
    )(lengths, *[in_vmem(x) for x in operands])


def attend_last(first_d, n_d, lengths, *operands):
    return pl.pallas_call(
        functools.partial(last_kernel, first_d, n_d),
        in_specs=[SMEM] + [VMEM] * len(operands),
        out_specs=[VMEM] * n_d,
        out_shape=[pltpu.VMEM((ROWS, PACKED), jnp.bfloat16)] * n_d,
        scratch_shapes=[pltpu.VMEM((n_d * BLOCK, HD), jnp.float32)] * 3,
        compiler_params=LARGE,
        name=f"attend_last_{first_d}",
    )(lengths, *[in_vmem(x) for x in operands])


def merged(parts, tick, live):
    levels = []
    for part_ref in parts:
        pieces = part_ref[:, 2 * WIDTH_DEV :].astype(jnp.float32)
        levels.append(
            pieces
            + pltpu.roll(pieces, 128 - HEADS_DEV, 1)
            + pltpu.roll(pieces, 128 - 2 * HEADS_DEV, 1)
        )
    top = functools.reduce(jnp.maximum, levels)
    shares = [jnp.exp2(level - top) for level in levels]
    inverse = 1.0 / functools.reduce(jnp.add, shares)
    shares = [share * inverse for share in shares]
    columns = []
    for h in range(HEADS_DEV):
        total = jnp.zeros((ROWS, HD), jnp.float32)
        column = tick * WIDTH_DEV + h * HD
        lane = tick * 3 * HEADS_DEV + h
        for part_ref, share in zip(parts, shares, strict=True):
            part = part_ref[:, column : column + HD].astype(jnp.float32)
            total = total + share[:, lane : lane + 1] * part
        columns.append(total)
    return jnp.where(live, jnp.concatenate(columns, 1), 0.0)


def live_rows(lengths_ref, tick):
    first = (lax.axis_index("cx") * NY + lax.axis_index("cy")) * ROWS
    row = first + lax.broadcasted_iota(jnp.int32, (ROWS, 1), 0)
    return row < lengths_ref[segment_of(tick)]


def merge_one_kernel(lengths_ref, rows_ref, *refs):
    parts, (residual_ref, sum_ref) = refs[:NY], refs[NY:]
    total = rows_ref[...].astype(jnp.float32) + merged(parts, 0, live_rows(lengths_ref, 0))
    sum_ref[...] = total
    residual_ref[...] = total.astype(jnp.bfloat16)


def merge_two_kernel(lengths_ref, *refs):
    parts, attended_ref = refs[:NY], refs[NY]
    attended_ref[...] = merged(parts, 1, live_rows(lengths_ref, 1))


def add_kernel(attended_ref, passed_ref, fresh_ref, sum_one_ref, sum_ref, squares_ref):
    first = lax.axis_index("section") == 0
    incoming = jnp.where(first, fresh_ref[...].astype(jnp.float32), passed_ref[...].astype(jnp.float32))
    total = incoming + attended_ref[...]
    sum_ref[...] = total
    ones = jnp.ones((8, WIDTH_DEV), jnp.float32)
    for tick, rows in enumerate((sum_one_ref[...], total)):
        squares = lax.dot_general(
            ones,
            rows * rows,
            (((1,), (1,)), ((), ())),
            precision=lax.Precision.HIGHEST,
            preferred_element_type=jnp.float32,
        )
        squares_ref[tick : tick + 1, :] = squares[:1]


def norm_kernel(squares_ref, sum_one_ref, sum_two_ref, gain_ref, residual_ref, normed_ref):
    gain = gain_ref[...].astype(jnp.float32)
    row = lax.broadcasted_iota(jnp.int32, (ROWS, ROWS), 0)
    lane = lax.broadcasted_iota(jnp.int32, (ROWS, ROWS), 1)
    for tick, sum_ref in enumerate((sum_one_ref, sum_two_ref)):
        scale = lax.rsqrt(squares_ref[tick : tick + 1, :] / FULL_WIDTH + EPSILON)
        column = jnp.sum(jnp.where(row == lane, scale, 0.0), axis=1, keepdims=True)
        residual_ref[tick] = sum_ref[...].astype(jnp.bfloat16)
        normed_ref[tick] = (sum_ref[...] * column * gain).astype(jnp.bfloat16)


def body(queries, key_rows, value_rows, section_rows, fresh_rows, norm_gain, segment_lengths):
    def along_x(value, by):
        return lax.ppermute(value, "cx", [(i, (i + by) % NX) for i in range(NX)])

    def across_y(value, d):
        return lax.ppermute(value, "cy", [(i, i ^ d) for i in range(NY)])

    k, v = key_rows[0], value_rows[0]
    k_below = along_x(k, 1)
    v_above = along_x(v, -1)
    q_own = jnp.broadcast_to(queries[:, 0], (NY, 2, ROWS, WIDTH_DEV))
    q_all = lax.all_to_all(q_own, "cy", 0, 0)
    v_below = along_x(v, 1)
    k_above = along_x(k, -1)
    k_far = along_x(k_below, 1)
    v_far = along_x(v_above, -1)

    state = attend_first(segment_lengths, q_all, k, v)
    state = attend_second(segment_lengths, q_all, k_below, v_below, *state)
    operands = (segment_lengths, q_all, k_above, v_above, k_far, v_far, *state)
    part_two, part_three = attend_last(2, 2, *operands)
    part_three = across_y(part_three, 3)
    part_two = across_y(part_two, 2)
    (part_one,) = attend_last(1, 1, *operands)
    part_one = across_y(part_one, 1)
    (part_own,) = attend_last(0, 1, *operands)
    parts = (part_own, part_one, part_two, part_three)

    rows_bf16 = pltpu.VMEM((ROWS, WIDTH_DEV), jnp.bfloat16)
    rows_f32 = pltpu.VMEM((ROWS, WIDTH_DEV), jnp.float32)
    parts = [in_vmem(part) for part in parts]
    residual_one, sum_one = pl.pallas_call(
        merge_one_kernel,
        in_specs=[SMEM] + [VMEM] * (1 + NY),
        out_specs=[VMEM] * 2,
        out_shape=[rows_bf16, rows_f32],
        compiler_params=SMALL,
        name="merge_one",
    )(segment_lengths, in_vmem(section_rows[0]), *parts)
    attended_two = pl.pallas_call(
        merge_two_kernel,
        in_specs=[SMEM] + [VMEM] * NY,
        out_specs=VMEM,
        out_shape=rows_f32,
        compiler_params=SMALL,
        name="merge_two",
    )(segment_lengths, *parts)
    count = lax.axis_size("section")
    passed = lax.ppermute(residual_one, "section", [(i, i + 1) for i in range(count - 1)])
    sum_two, squares = pl.pallas_call(
        add_kernel,
        in_specs=[VMEM] * 4,
        out_specs=[VMEM] * 2,
        out_shape=[rows_f32, pltpu.VMEM((2, ROWS), jnp.float32)],
        compiler_params=SMALL,
        name="add",
    )(*[in_vmem(x) for x in (attended_two, passed, fresh_rows, sum_one)])
    squares = lax.psum(squares, "tp")
    residual, normed = pl.pallas_call(
        norm_kernel,
        in_specs=[VMEM] * 4,
        out_specs=[VMEM] * 2,
        out_shape=[jax.ShapeDtypeStruct((2, ROWS, WIDTH_DEV), jnp.bfloat16)] * 2,
        compiler_params=SMALL,
        name="norm",
    )(in_vmem(squares), in_vmem(sum_one), in_vmem(sum_two), in_vmem(norm_gain))
    return residual[:, None], normed[:, None]


def solution(mesh):
    grid = Mesh(mesh.devices.reshape(8, NX, NY, 4), ("section", "cx", "cy", "tp"))
    cp = ("cx", "cy")
    in_specs = (
        P(None, "section", cp, "tp"),
        P("section", cp, "tp"),
        P("section", cp, "tp"),
        P("section", cp, "tp"),
        P(cp, "tp"),
        P("section", "tp"),
        P(),
    )
    out_specs = (P(None, "section", cp, "tp"), P(None, "section", cp, "tp"))
    return jax.shard_map(body, mesh=grid, in_specs=in_specs, out_specs=out_specs, check_vma=False)
```

```python
import functools

import jax
import jax.numpy as jnp
import numpy as np
from jax import lax
from jax.experimental import pallas as pl
from jax.experimental.pallas import tpu as pltpu
from jax.sharding import Mesh
from jax.sharding import PartitionSpec as P

HD = 128
NX, NY = 4, 4
HEADS_DEV = 8
ROWS = 32
WIDTH_DEV = HEADS_DEV * HD
KEYS = 1536
CTX = KEYS * NX * NY
N_SEG = 9
FULL_WIDTH = 4096
PACKED = 2 * WIDTH_DEV + 128
BLOCK = 2 * HEADS_DEV * ROWS
HALF = 2 * BLOCK
NEGATIVE = -1e30
FLOOR = -1e28
EMPTY = (0.0, FLOOR, 0.0)
OWN_TILE = 512
TINY = 1e-30
EPSILON = 1e-05
LOG2_SCALE = float(np.log2(np.e) / np.sqrt(HD))
VMEM_LIMIT = 24 * 2**20
LARGE = pltpu.CompilerParams(vmem_limit_bytes=VMEM_LIMIT)
SMALL = pltpu.CompilerParams(vmem_limit_bytes=4 * 2**20)


SMEM = pl.BlockSpec(memory_space=pltpu.SMEM)
VMEM = pl.BlockSpec(memory_space=pltpu.VMEM)
ANY = pl.BlockSpec(memory_space=pl.ANY)


def segment_of(tick):
    return 7 - lax.axis_index("section") + tick


def segment_start(lengths_ref, segment):
    start = jnp.int32(CTX)
    for j in range(N_SEG):
        start = start - jnp.where(j >= segment, lengths_ref[j], 0)
    return start


def update(state, q, k_ref, v_ref, last_offset, length):
    out, top, total = state
    for begin in range(0, KEYS, length):
        tile = slice(begin, begin + length)
        s = lax.dot_general(
            q, k_ref[tile], (((1,), (1,)), ((), ())), preferred_element_type=jnp.float32
        )
        if last_offset is not None:
            offset = begin + lax.broadcasted_iota(jnp.int32, (1, length), 1)
            s = jnp.where(offset <= last_offset, s, NEGATIVE)
        part = s[:, :HD]
        for u in range(1, length // HD):
            part = jnp.maximum(part, s[:, u * HD : (u + 1) * HD])
        tile_top = jnp.max(part, axis=1, keepdims=True) * LOG2_SCALE
        new_top = jnp.maximum(top, jnp.broadcast_to(tile_top, top.shape))
        groups = [
            jnp.exp2(s[:, u * HD : (u + 1) * HD] * LOG2_SCALE - new_top)
            for u in range(length // HD)
        ]
        lane_sum = functools.reduce(jnp.add, groups)
        p = jnp.concatenate([group.astype(jnp.bfloat16) for group in groups], 1)
        mixed = jnp.dot(p, v_ref[tile], preferred_element_type=jnp.float32)
        rescale = jnp.exp2(top - new_top)
        out = out * rescale + mixed
        total = total * rescale + lane_sum
        top = new_top
    return out, top, total


def finished(out_ref, top_ref, total_ref):
    total = jnp.maximum(jnp.sum(total_ref[...], axis=1, keepdims=True), TINY)
    return out_ref[...] * (1.0 / total), top_ref[...] + jnp.log2(total)


def write_packed(state, outs):
    out, level = state
    out = out.astype(jnp.bfloat16)
    lane = lax.broadcasted_iota(jnp.int32, (ROWS, 128), 1)
    head = lane % HEADS_DEV
    piece = lane % (3 * HEADS_DEV) // HEADS_DEV
    for i, o_ref in enumerate(outs):
        levels = jnp.zeros((ROWS, 128), jnp.float32)
        for tick in range(2):
            mine = lane // (3 * HEADS_DEV) == tick
            for h in range(HEADS_DEV):
                at = ((i * 2 + tick) * HEADS_DEV + h) * ROWS
                column = tick * WIDTH_DEV + h * HD
                o_ref[:, column : column + HD] = out[at : at + ROWS]
                levels = jnp.where(jnp.logical_and(mine, head == h), level[at : at + ROWS], levels)
        high = levels.astype(jnp.bfloat16).astype(jnp.float32)
        middle = (levels - high).astype(jnp.bfloat16).astype(jnp.float32)
        low = levels - high - middle
        pieces = jnp.where(piece == 0, high, jnp.where(piece == 1, middle, low))
        o_ref[:, 2 * WIDTH_DEV :] = pieces.astype(jnp.bfloat16)


def attend_rows(first_d, n_d, shift, lengths_ref, q_ref, k_ref, v_ref, state, started=True):
    cx = lax.axis_index("cx")
    cy = lax.axis_index("cy")
    base = cx * NY * ROWS - ((cx + shift) % NX * NY + cy) * KEYS
    least = [segment_start(lengths_ref, segment_of(tick)) + base for tick in range(2)]
    full = jnp.minimum(least[0], least[1]) >= KEYS - 1
    none = jnp.maximum(least[0], least[1]) + NY * ROWS - 1 < 0

    def run(masked):
        q = jnp.concatenate(
            [
                q_ref[cy ^ (first_d + i), tick, :, h * HD : (h + 1) * HD]
                for i in range(n_d)
                for tick in range(2)
                for h in range(HEADS_DEV)
            ],
            0,
        )
        last_offset = None
        if masked:
            row_id = lax.broadcasted_iota(jnp.int32, (n_d * BLOCK, 1), 0)
            owner = (first_d + row_id // BLOCK) ^ cy
            second = row_id // (BLOCK // 2) % 2 == 1
            last_offset = jnp.where(second, least[1], least[0]) + owner * ROWS + row_id % ROWS
        if started:
            held = tuple(ref[...] for ref in state)
        else:
            held = tuple(jnp.full((n_d * BLOCK, HD), x, jnp.float32) for x in EMPTY)
        length = KEYS if started else OWN_TILE
        result = update(held, q, k_ref, v_ref, last_offset, length)
        for ref, value in zip(state, result, strict=True):
            ref[...] = value

    @pl.when(full)
    def _():
        run(False)

    @pl.when(jnp.logical_not(jnp.logical_or(full, none)))
    def _():
        run(True)

    if not started:

        @pl.when(none)
        def _():
            for ref, value in zip(state, EMPTY, strict=True):
                ref[...] = jnp.full(ref.shape, value, jnp.float32)


def first_kernel(lengths_ref, q_ref, k_ref, v_ref, out_ref, top_ref, total_ref):
    def one(half, _):
        state = [ref.at[half] for ref in (out_ref, top_ref, total_ref)]
        attend_rows(2 * half, 2, 0, lengths_ref, q_ref, k_ref, v_ref, state, started=False)

    lax.fori_loop(0, 2, one, None)


def second_kernel(lengths_ref, q_ref, k_ref, v_ref, *refs):
    inputs, outs = refs[:3], refs[3:]

    def one(half, _):
        for source, target in zip(inputs, outs, strict=True):
            target[half] = source[half]
        state = [ref.at[half] for ref in outs]
        attend_rows(2 * half, 2, NX - 1, lengths_ref, q_ref, k_ref, v_ref, state)

    lax.fori_loop(0, 2, one, None)


def above_kernel(lengths_ref, q_ref, k_ref, v_ref, *refs):
    inputs, outs = refs[:3], refs[3:]
    for source, target in zip(inputs, outs, strict=True):
        target[...] = source[1]
    attend_rows(2, 2, 1, lengths_ref, q_ref, k_ref, v_ref, outs)


def far_kernel(lengths_ref, q_ref, k_ref, v_ref, *refs):
    inputs, outs, state = refs[:3], refs[3:5], refs[5:]
    for source, target in zip(inputs, state, strict=True):
        target[...] = source[...]
    attend_rows(2, 2, 2, lengths_ref, q_ref, k_ref, v_ref, state)
    write_packed(finished(*state), outs)


def near_kernel(d, *refs):
    lengths_ref, q_ref, k_above, v_above, k_far, v_far = refs[:6]
    inputs, o_ref, state = refs[6:9], refs[9], refs[10:]
    for source, target in zip(inputs, state, strict=True):
        target[...] = source[0, d * BLOCK : (d + 1) * BLOCK]
    attend_rows(d, 1, 1, lengths_ref, q_ref, k_above, v_above, state)
    attend_rows(d, 1, 2, lengths_ref, q_ref, k_far, v_far, state)
    write_packed(finished(*state), [o_ref])


def in_vmem(x):
    return pltpu.with_memory_space_constraint(x, pltpu.VMEM)


def in_hbm(x):
    return pltpu.with_memory_space_constraint(x, pltpu.HBM)


def attend(kernel, name, out_shape, scratch_rows, lengths, *operands):
    return pl.pallas_call(
        kernel,
        in_specs=[SMEM] + [VMEM] * len(operands),
        out_specs=[VMEM] * len(out_shape),
        out_shape=out_shape,
        scratch_shapes=[pltpu.VMEM((scratch_rows, HD), jnp.float32)] * 3 if scratch_rows else [],
        compiler_params=LARGE,
        name=name,
    )(lengths, *[in_vmem(x) for x in operands])


def merged(parts, tick, live):
    levels = []
    for part_ref in parts:
        pieces = part_ref[:, 2 * WIDTH_DEV :].astype(jnp.float32)
        levels.append(
            pieces
            + pltpu.roll(pieces, 128 - HEADS_DEV, 1)
            + pltpu.roll(pieces, 128 - 2 * HEADS_DEV, 1)
        )
    top = functools.reduce(jnp.maximum, levels)
    shares = [jnp.exp2(level - top) for level in levels]
    inverse = 1.0 / functools.reduce(jnp.add, shares)
    shares = [share * inverse for share in shares]
    columns = []
    for h in range(HEADS_DEV):
        total = jnp.zeros((ROWS, HD), jnp.float32)
        column = tick * WIDTH_DEV + h * HD
        lane = tick * 3 * HEADS_DEV + h
        for part_ref, share in zip(parts, shares, strict=True):
            part = part_ref[:, column : column + HD].astype(jnp.float32)
            total = total + share[:, lane : lane + 1] * part
        columns.append(total)
    return jnp.where(live, jnp.concatenate(columns, 1), 0.0)


def live_rows(lengths_ref, tick):
    first = (lax.axis_index("cx") * NY + lax.axis_index("cy")) * ROWS
    row = first + lax.broadcasted_iota(jnp.int32, (ROWS, 1), 0)
    return row < lengths_ref[segment_of(tick)]


def merge_one_kernel(lengths_ref, rows_ref, *refs):
    parts, (residual_ref, sum_ref) = refs[:NY], refs[NY:]
    total = rows_ref[...].astype(jnp.float32) + merged(parts, 0, live_rows(lengths_ref, 0))
    sum_ref[...] = total
    residual_ref[...] = total.astype(jnp.bfloat16)


def merge_two_kernel(lengths_ref, *refs):
    parts, attended_ref = refs[:NY], refs[NY]
    attended_ref[...] = merged(parts, 1, live_rows(lengths_ref, 1))


def add_kernel(attended_ref, passed_ref, fresh_ref, sum_one_ref, sum_ref, squares_ref):
    first = lax.axis_index("section") == 0
    incoming = jnp.where(first, fresh_ref[...].astype(jnp.float32), passed_ref[...].astype(jnp.float32))
    total = incoming + attended_ref[...]
    sum_ref[...] = total
    ones = jnp.ones((8, WIDTH_DEV), jnp.float32)
    for tick, rows in enumerate((sum_one_ref[...], total)):
        squares = lax.dot_general(
            ones,
            rows * rows,
            (((1,), (1,)), ((), ())),
            precision=lax.Precision.HIGHEST,
            preferred_element_type=jnp.float32,
        )
        squares_ref[tick : tick + 1, :] = squares[:1]


def norm_kernel(squares_ref, sum_one_ref, sum_two_ref, gain_ref, residual_ref, normed_ref):
    gain = gain_ref[...].astype(jnp.float32)
    row = lax.broadcasted_iota(jnp.int32, (ROWS, ROWS), 0)
    lane = lax.broadcasted_iota(jnp.int32, (ROWS, ROWS), 1)
    for tick, sum_ref in enumerate((sum_one_ref, sum_two_ref)):
        squares = functools.reduce(
            jnp.add, [squares_ref[i, tick : tick + 1, :] for i in range(squares_ref.shape[0])]
        )
        scale = lax.rsqrt(squares / FULL_WIDTH + EPSILON)
        column = jnp.sum(jnp.where(row == lane, scale, 0.0), axis=1, keepdims=True)
        residual_ref[tick] = sum_ref[...].astype(jnp.bfloat16)
        normed_ref[tick] = (sum_ref[...] * column * gain).astype(jnp.bfloat16)


def body(queries, key_rows, value_rows, section_rows, fresh_rows, norm_gain, segment_lengths):
    def along_x(value, by):
        return lax.ppermute(value, "cx", [(i, (i + by) % NX) for i in range(NX)])

    def across_y(value, d):
        return lax.ppermute(value, "cy", [(i, i ^ d) for i in range(NY)])

    k, v = key_rows[0], value_rows[0]
    k_below = along_x(k, 1)
    v_above = along_x(v, -1)
    q_own = jnp.broadcast_to(queries[:, 0], (NY, 2, ROWS, WIDTH_DEV))
    q_all = lax.all_to_all(q_own, "cy", 0, 0)
    v_below = along_x(v, 1)
    k_above = along_x(k, -1)
    k_far = along_x(k_below, 1)
    v_far = along_x(v_above, -1)

    both = [pltpu.VMEM((2, HALF, HD), jnp.float32)] * 3
    one = [pltpu.VMEM((HALF, HD), jnp.float32)] * 3
    packed = pltpu.VMEM((ROWS, PACKED), jnp.bfloat16)
    common = (segment_lengths, q_all)
    state = attend(first_kernel, "attend_own", both, 0, *common, k, v)
    state = attend(second_kernel, "attend_below", both, 0, *common, k_below, v_below, *state)
    upper = attend(above_kernel, "attend_above", one, 0, *common, k_above, v_above, *state)
    part_two, part_three = attend(
        far_kernel, "attend_far", [packed] * 2, HALF, *common, k_far, v_far, *upper
    )
    part_three = across_y(part_three, 3)
    part_two = across_y(part_two, 2)
    near = [
        attend(
            functools.partial(near_kernel, d),
            f"attend_near_{d}",
            [packed],
            BLOCK,
            *common,
            k_above,
            v_above,
            k_far,
            v_far,
            *state,
        )[0]
        for d in range(2)
    ]
    parts = (near[0], across_y(near[1], 1), part_two, part_three)

    rows_bf16 = pltpu.VMEM((ROWS, WIDTH_DEV), jnp.bfloat16)
    rows_f32 = pltpu.VMEM((ROWS, WIDTH_DEV), jnp.float32)
    parts = [in_vmem(part) for part in parts]
    residual_one, sum_one = pl.pallas_call(
        merge_one_kernel,
        in_specs=[SMEM] + [VMEM] * (1 + NY),
        out_specs=[VMEM] * 2,
        out_shape=[rows_bf16, rows_f32],
        compiler_params=SMALL,
        name="merge_one",
    )(segment_lengths, in_vmem(section_rows[0]), *parts)
    attended_two = pl.pallas_call(
        merge_two_kernel,
        in_specs=[SMEM] + [VMEM] * NY,
        out_specs=VMEM,
        out_shape=rows_f32,
        compiler_params=SMALL,
        name="merge_two",
    )(segment_lengths, *parts)
    count = lax.axis_size("section")
    passed = lax.ppermute(residual_one, "section", [(i, i + 1) for i in range(count - 1)])
    sum_two, squares = pl.pallas_call(
        add_kernel,
        in_specs=[VMEM] * 4,
        out_specs=[VMEM] * 2,
        out_shape=[rows_f32, pltpu.VMEM((2, ROWS), jnp.float32)],
        compiler_params=SMALL,
        name="add",
    )(*[in_vmem(x) for x in (attended_two, passed, fresh_rows, sum_one)])
    squares = lax.all_gather(squares, "tp")
    residual, normed = pl.pallas_call(
        norm_kernel,
        in_specs=[VMEM] * 4,
        out_specs=[VMEM] * 2,
        out_shape=[jax.ShapeDtypeStruct((2, ROWS, WIDTH_DEV), jnp.bfloat16)] * 2,
        compiler_params=SMALL,
        name="norm",
    )(in_vmem(squares), in_vmem(sum_one), in_vmem(sum_two), in_vmem(norm_gain))
    return residual[:, None], normed[:, None]


def solution(mesh):
    grid = Mesh(mesh.devices.reshape(8, NX, NY, 4), ("section", "cx", "cy", "tp"))
    cp = ("cx", "cy")
    in_specs = (
        P(None, "section", cp, "tp"),
        P("section", cp, "tp"),
        P("section", cp, "tp"),
        P("section", cp, "tp"),
        P(cp, "tp"),
        P("section", "tp"),
        P(),
    )
    out_specs = (P(None, "section", cp, "tp"), P(None, "section", cp, "tp"))
    return jax.shard_map(body, mesh=grid, in_specs=in_specs, out_specs=out_specs, check_vma=False)
```

```python
import functools

import jax
import jax.numpy as jnp
import numpy as np
from jax import lax
from jax.experimental import pallas as pl
from jax.experimental.pallas import tpu as pltpu
from jax.sharding import Mesh
from jax.sharding import PartitionSpec as P

HD = 128
NX, NY = 4, 4
HEADS_DEV = 8
ROWS = 32
WIDTH_DEV = HEADS_DEV * HD
KEYS = 1536
CTX = KEYS * NX * NY
N_SEG = 9
FULL_WIDTH = 4096
PACKED = 2 * WIDTH_DEV + 128
BLOCK = 2 * HEADS_DEV * ROWS
HALF = 2 * BLOCK
NEGATIVE = -1e30
FLOOR = -1e28
EMPTY = (0.0, FLOOR, 0.0)
OWN_TILE = 512
TINY = 1e-30
EPSILON = 1e-05
LOG2_SCALE = float(np.log2(np.e) / np.sqrt(HD))
VMEM_LIMIT = 24 * 2**20
LARGE = pltpu.CompilerParams(vmem_limit_bytes=VMEM_LIMIT)
SMALL = pltpu.CompilerParams(vmem_limit_bytes=4 * 2**20)


SMEM = pl.BlockSpec(memory_space=pltpu.SMEM)
VMEM = pl.BlockSpec(memory_space=pltpu.VMEM)
ANY = pl.BlockSpec(memory_space=pl.ANY)


def segment_of(tick):
    return 7 - lax.axis_index("section") + tick


def segment_start(lengths_ref, segment):
    start = jnp.int32(CTX)
    for j in range(N_SEG):
        start = start - jnp.where(j >= segment, lengths_ref[j], 0)
    return start


def update(state, q, k_ref, v_ref, last_offset, length):
    out, top, total = state
    for begin in range(0, KEYS, length):
        tile = slice(begin, begin + length)
        s = lax.dot_general(
            q, k_ref[tile], (((1,), (1,)), ((), ())), preferred_element_type=jnp.float32
        )
        if last_offset is not None:
            offset = begin + lax.broadcasted_iota(jnp.int32, (1, length), 1)
            s = jnp.where(offset <= last_offset, s, NEGATIVE)
        part = s[:, :HD]
        for u in range(1, length // HD):
            part = jnp.maximum(part, s[:, u * HD : (u + 1) * HD])
        tile_top = jnp.max(part, axis=1, keepdims=True) * LOG2_SCALE
        new_top = jnp.maximum(top, jnp.broadcast_to(tile_top, top.shape))
        groups = [
            jnp.exp2(s[:, u * HD : (u + 1) * HD] * LOG2_SCALE - new_top)
            for u in range(length // HD)
        ]
        lane_sum = functools.reduce(jnp.add, groups)
        p = jnp.concatenate([group.astype(jnp.bfloat16) for group in groups], 1)
        mixed = jnp.dot(p, v_ref[tile], preferred_element_type=jnp.float32)
        rescale = jnp.exp2(top - new_top)
        out = out * rescale + mixed
        total = total * rescale + lane_sum
        top = new_top
    return out, top, total


def finished(out_ref, top_ref, total_ref):
    total = jnp.maximum(jnp.sum(total_ref[...], axis=1, keepdims=True), TINY)
    return out_ref[...] * (1.0 / total), top_ref[...] + jnp.log2(total)


def write_packed(state, outs):
    out, level = state
    out = out.astype(jnp.bfloat16)
    lane = lax.broadcasted_iota(jnp.int32, (ROWS, 128), 1)
    head = lane % HEADS_DEV
    piece = lane % (3 * HEADS_DEV) // HEADS_DEV
    for i, o_ref in enumerate(outs):
        levels = jnp.zeros((ROWS, 128), jnp.float32)
        for tick in range(2):
            mine = lane // (3 * HEADS_DEV) == tick
            for h in range(HEADS_DEV):
                at = ((i * 2 + tick) * HEADS_DEV + h) * ROWS
                column = tick * WIDTH_DEV + h * HD
                o_ref[:, column : column + HD] = out[at : at + ROWS]
                levels = jnp.where(jnp.logical_and(mine, head == h), level[at : at + ROWS], levels)
        high = levels.astype(jnp.bfloat16).astype(jnp.float32)
        middle = (levels - high).astype(jnp.bfloat16).astype(jnp.float32)
        low = levels - high - middle
        pieces = jnp.where(piece == 0, high, jnp.where(piece == 1, middle, low))
        o_ref[:, 2 * WIDTH_DEV :] = pieces.astype(jnp.bfloat16)


def attend_rows(first_d, n_d, shift, lengths_ref, q_ref, k_ref, v_ref, state, started=True):
    cx = lax.axis_index("cx")
    cy = lax.axis_index("cy")
    base = cx * NY * ROWS - ((cx + shift) % NX * NY + cy) * KEYS
    least = [segment_start(lengths_ref, segment_of(tick)) + base for tick in range(2)]
    full = jnp.minimum(least[0], least[1]) >= KEYS - 1
    none = jnp.maximum(least[0], least[1]) + NY * ROWS - 1 < 0

    def run(masked):
        q = jnp.concatenate(
            [
                q_ref[cy ^ (first_d + i), tick, :, h * HD : (h + 1) * HD]
                for i in range(n_d)
                for tick in range(2)
                for h in range(HEADS_DEV)
            ],
            0,
        )
        last_offset = None
        if masked:
            row_id = lax.broadcasted_iota(jnp.int32, (n_d * BLOCK, 1), 0)
            owner = (first_d + row_id // BLOCK) ^ cy
            second = row_id // (BLOCK // 2) % 2 == 1
            last_offset = jnp.where(second, least[1], least[0]) + owner * ROWS + row_id % ROWS
        if started:
            held = tuple(ref[...] for ref in state)
        else:
            held = tuple(jnp.full((n_d * BLOCK, HD), x, jnp.float32) for x in EMPTY)
        length = KEYS if started else OWN_TILE
        result = update(held, q, k_ref, v_ref, last_offset, length)
        for ref, value in zip(state, result, strict=True):
            ref[...] = value

    @pl.when(full)
    def _():
        run(False)

    @pl.when(jnp.logical_not(jnp.logical_or(full, none)))
    def _():
        run(True)

    if not started:

        @pl.when(none)
        def _():
            for ref, value in zip(state, EMPTY, strict=True):
                ref[...] = jnp.full(ref.shape, value, jnp.float32)


def first_kernel(lengths_ref, q_ref, k_ref, v_ref, out_ref, top_ref, total_ref):
    def one(half, _):
        state = [ref.at[half] for ref in (out_ref, top_ref, total_ref)]
        attend_rows(2 * half, 2, 0, lengths_ref, q_ref, k_ref, v_ref, state, started=False)

    lax.fori_loop(0, 2, one, None)


def second_kernel(lengths_ref, q_ref, k_ref, v_ref, *refs):
    inputs, outs = refs[:3], refs[3:]

    def one(half, _):
        for source, target in zip(inputs, outs, strict=True):
            target[half] = source[half]
        state = [ref.at[half] for ref in outs]
        attend_rows(2 * half, 2, NX - 1, lengths_ref, q_ref, k_ref, v_ref, state)

    lax.fori_loop(0, 2, one, None)


def above_kernel(lengths_ref, q_ref, k_ref, v_ref, *refs):
    inputs, outs = refs[:3], refs[3:]
    for source, target in zip(inputs, outs, strict=True):
        target[...] = source[1]
    attend_rows(2, 2, 1, lengths_ref, q_ref, k_ref, v_ref, outs)


def far_kernel(lengths_ref, q_ref, k_ref, v_ref, *refs):
    inputs, outs, state = refs[:3], refs[3:5], refs[5:]
    for source, target in zip(inputs, state, strict=True):
        target[...] = source[...]
    attend_rows(2, 2, 2, lengths_ref, q_ref, k_ref, v_ref, state)
    write_packed(finished(*state), outs)


def near_kernel(d, *refs):
    lengths_ref, q_ref, k_above, v_above, k_far, v_far = refs[:6]
    inputs, o_ref, state = refs[6:9], refs[9], refs[10:]
    for source, target in zip(inputs, state, strict=True):
        target[...] = source[0, d * BLOCK : (d + 1) * BLOCK]
    attend_rows(d, 1, 1, lengths_ref, q_ref, k_above, v_above, state)
    attend_rows(d, 1, 2, lengths_ref, q_ref, k_far, v_far, state)
    write_packed(finished(*state), [o_ref])


def in_vmem(x):
    return pltpu.with_memory_space_constraint(x, pltpu.VMEM)


def in_hbm(x):
    return pltpu.with_memory_space_constraint(x, pltpu.HBM)


def attend(kernel, name, out_shape, scratch_rows, lengths, *operands):
    return pl.pallas_call(
        kernel,
        in_specs=[SMEM] + [VMEM] * len(operands),
        out_specs=[VMEM] * len(out_shape),
        out_shape=out_shape,
        scratch_shapes=[pltpu.VMEM((scratch_rows, HD), jnp.float32)] * 3 if scratch_rows else [],
        compiler_params=LARGE,
        name=name,
    )(lengths, *[in_vmem(x) for x in operands])


def merged(parts, tick, live):
    levels = []
    for part_ref in parts:
        pieces = part_ref[:, 2 * WIDTH_DEV :].astype(jnp.float32)
        levels.append(
            pieces
            + pltpu.roll(pieces, 128 - HEADS_DEV, 1)
            + pltpu.roll(pieces, 128 - 2 * HEADS_DEV, 1)
        )
    top = functools.reduce(jnp.maximum, levels)
    shares = [jnp.exp2(level - top) for level in levels]
    inverse = 1.0 / functools.reduce(jnp.add, shares)
    shares = [share * inverse for share in shares]
    columns = []
    for h in range(HEADS_DEV):
        total = jnp.zeros((ROWS, HD), jnp.float32)
        column = tick * WIDTH_DEV + h * HD
        lane = tick * 3 * HEADS_DEV + h
        for part_ref, share in zip(parts, shares, strict=True):
            part = part_ref[:, column : column + HD].astype(jnp.float32)
            total = total + share[:, lane : lane + 1] * part
        columns.append(total)
    return jnp.where(live, jnp.concatenate(columns, 1), 0.0)


def live_rows(lengths_ref, tick):
    first = (lax.axis_index("cx") * NY + lax.axis_index("cy")) * ROWS
    row = first + lax.broadcasted_iota(jnp.int32, (ROWS, 1), 0)
    return row < lengths_ref[segment_of(tick)]


def merge_one_kernel(lengths_ref, rows_ref, *refs):
    parts, (residual_ref, sum_ref) = refs[:NY], refs[NY:]
    total = rows_ref[...].astype(jnp.float32) + merged(parts, 0, live_rows(lengths_ref, 0))
    sum_ref[...] = total
    residual_ref[...] = total.astype(jnp.bfloat16)


def merge_two_kernel(lengths_ref, *refs):
    parts, attended_ref = refs[:NY], refs[NY]
    attended_ref[...] = merged(parts, 1, live_rows(lengths_ref, 1))


def add_kernel(attended_ref, passed_ref, fresh_ref, sum_one_ref, sum_ref, squares_ref):
    first = lax.axis_index("section") == 0
    incoming = jnp.where(first, fresh_ref[...].astype(jnp.float32), passed_ref[...].astype(jnp.float32))
    total = incoming + attended_ref[...]
    sum_ref[...] = total
    ones = jnp.ones((8, WIDTH_DEV), jnp.float32)
    for tick, rows in enumerate((sum_one_ref[...], total)):
        squares = lax.dot_general(
            ones,
            rows * rows,
            (((1,), (1,)), ((), ())),
            precision=lax.Precision.HIGHEST,
            preferred_element_type=jnp.float32,
        )
        squares_ref[tick : tick + 1, :] = squares[:1]


def norm_kernel(squares_ref, sum_one_ref, sum_two_ref, gain_ref, residual_ref, normed_ref):
    gain = gain_ref[...].astype(jnp.float32)
    row = lax.broadcasted_iota(jnp.int32, (ROWS, ROWS), 0)
    lane = lax.broadcasted_iota(jnp.int32, (ROWS, ROWS), 1)
    for tick, sum_ref in enumerate((sum_one_ref, sum_two_ref)):
        squares = functools.reduce(
            jnp.add, [squares_ref[i, tick : tick + 1, :] for i in range(squares_ref.shape[0])]
        )
        scale = lax.rsqrt(squares / FULL_WIDTH + EPSILON)
        column = jnp.sum(jnp.where(row == lane, scale, 0.0), axis=1, keepdims=True)
        residual_ref[tick] = sum_ref[...].astype(jnp.bfloat16)
        normed_ref[tick] = (sum_ref[...] * column * gain).astype(jnp.bfloat16)


def body(queries, key_rows, value_rows, section_rows, fresh_rows, norm_gain, segment_lengths):
    def along_x(value, by):
        return lax.ppermute(value, "cx", [(i, (i + by) % NX) for i in range(NX)])

    def across_y(value, d):
        return lax.ppermute(value, "cy", [(i, i ^ d) for i in range(NY)])

    k, v = key_rows[0], value_rows[0]
    k_below = along_x(k, 1)
    v_above = along_x(v, -1)
    q_own = jnp.broadcast_to(queries[:, 0], (NY, 2, ROWS, WIDTH_DEV))
    q_all = lax.all_to_all(q_own, "cy", 0, 0)
    v_next, k_below = lax.optimization_barrier((v, k_below))
    v_below = along_x(v_next, 1)
    k_above = along_x(k, -1)
    k_far = along_x(k_below, 1)
    v_far = along_x(v_above, -1)

    both = [pltpu.VMEM((2, HALF, HD), jnp.float32)] * 3
    one = [pltpu.VMEM((HALF, HD), jnp.float32)] * 3
    packed = pltpu.VMEM((ROWS, PACKED), jnp.bfloat16)
    common = (segment_lengths, q_all)
    state = attend(first_kernel, "attend_own", both, 0, *common, k, v)
    state = attend(second_kernel, "attend_below", both, 0, *common, k_below, v_below, *state)
    upper = attend(above_kernel, "attend_above", one, 0, *common, k_above, v_above, *state)
    part_two, part_three = attend(
        far_kernel, "attend_far", [packed] * 2, HALF, *common, k_far, v_far, *upper
    )
    part_three = across_y(part_three, 3)
    part_two = across_y(part_two, 2)
    near = [
        attend(
            functools.partial(near_kernel, d),
            f"attend_near_{d}",
            [packed],
            BLOCK,
            *common,
            k_above,
            v_above,
            k_far,
            v_far,
            *state,
        )[0]
        for d in range(2)
    ]
    parts = (near[0], across_y(near[1], 1), part_two, part_three)

    rows_bf16 = pltpu.VMEM((ROWS, WIDTH_DEV), jnp.bfloat16)
    rows_f32 = pltpu.VMEM((ROWS, WIDTH_DEV), jnp.float32)
    parts = [in_vmem(part) for part in parts]
    residual_one, sum_one = pl.pallas_call(
        merge_one_kernel,
        in_specs=[SMEM] + [VMEM] * (1 + NY),
        out_specs=[VMEM] * 2,
        out_shape=[rows_bf16, rows_f32],
        compiler_params=SMALL,
        name="merge_one",
    )(segment_lengths, in_vmem(section_rows[0]), *parts)
    attended_two = pl.pallas_call(
        merge_two_kernel,
        in_specs=[SMEM] + [VMEM] * NY,
        out_specs=VMEM,
        out_shape=rows_f32,
        compiler_params=SMALL,
        name="merge_two",
    )(segment_lengths, *parts)
    count = lax.axis_size("section")
    passed = lax.ppermute(residual_one, "section", [(i, i + 1) for i in range(count - 1)])
    sum_two, squares = pl.pallas_call(
        add_kernel,
        in_specs=[VMEM] * 4,
        out_specs=[VMEM] * 2,
        out_shape=[rows_f32, pltpu.VMEM((2, ROWS), jnp.float32)],
        compiler_params=SMALL,
        name="add",
    )(*[in_vmem(x) for x in (attended_two, passed, fresh_rows, sum_one)])
    squares = lax.all_gather(squares, "tp")
    residual, normed = pl.pallas_call(
        norm_kernel,
        in_specs=[VMEM] * 4,
        out_specs=[VMEM] * 2,
        out_shape=[jax.ShapeDtypeStruct((2, ROWS, WIDTH_DEV), jnp.bfloat16)] * 2,
        compiler_params=SMALL,
        name="norm",
    )(in_vmem(squares), in_vmem(sum_one), in_vmem(sum_two), in_vmem(norm_gain))
    return residual[:, None], normed[:, None]


def solution(mesh):
    grid = Mesh(mesh.devices.reshape(8, NX, NY, 4), ("section", "cx", "cy", "tp"))
    cp = ("cx", "cy")
    in_specs = (
        P(None, "section", cp, "tp"),
        P("section", cp, "tp"),
        P("section", cp, "tp"),
        P("section", cp, "tp"),
        P(cp, "tp"),
        P("section", "tp"),
        P(),
    )
    out_specs = (P(None, "section", cp, "tp"), P(None, "section", cp, "tp"))
    return jax.shard_map(body, mesh=grid, in_specs=in_specs, out_specs=out_specs, check_vma=False)
```

```python
import functools

import jax
import jax.numpy as jnp
import numpy as np
from jax import lax
from jax.experimental import pallas as pl
from jax.experimental.pallas import tpu as pltpu
from jax.sharding import Mesh
from jax.sharding import PartitionSpec as P

HD = 128
NX, NY = 4, 4
HEADS_DEV = 8
ROWS = 32
WIDTH_DEV = HEADS_DEV * HD
KEYS = 1536
CTX = KEYS * NX * NY
N_SEG = 9
FULL_WIDTH = 4096
PACKED = 2 * WIDTH_DEV + 128
BLOCK = 2 * HEADS_DEV * ROWS
HALF = 2 * BLOCK
NEGATIVE = -1e30
FLOOR = -1e28
EMPTY = (0.0, FLOOR, 0.0)
OWN_TILE = 512
TINY = 1e-30
EPSILON = 1e-05
LOG2_SCALE = float(np.log2(np.e) / np.sqrt(HD))
VMEM_LIMIT = 24 * 2**20
LARGE = pltpu.CompilerParams(vmem_limit_bytes=VMEM_LIMIT)
SMALL = pltpu.CompilerParams(vmem_limit_bytes=4 * 2**20)


SMEM = pl.BlockSpec(memory_space=pltpu.SMEM)
VMEM = pl.BlockSpec(memory_space=pltpu.VMEM)
ANY = pl.BlockSpec(memory_space=pl.ANY)


def segment_of(tick):
    return 7 - lax.axis_index("section") + tick


def segment_start(lengths_ref, segment):
    start = jnp.int32(CTX)
    for j in range(N_SEG):
        start = start - jnp.where(j >= segment, lengths_ref[j], 0)
    return start


def update(state, q, k_ref, v_ref, last_offset, length):
    out, top, total = state
    for begin in range(0, KEYS, length):
        tile = slice(begin, begin + length)
        s = lax.dot_general(
            q, k_ref[tile], (((1,), (1,)), ((), ())), preferred_element_type=jnp.float32
        )
        if last_offset is not None:
            offset = begin + lax.broadcasted_iota(jnp.int32, (1, length), 1)
            s = jnp.where(offset <= last_offset, s, NEGATIVE)
        part = s[:, :HD]
        for u in range(1, length // HD):
            part = jnp.maximum(part, s[:, u * HD : (u + 1) * HD])
        tile_top = jnp.max(part, axis=1, keepdims=True) * LOG2_SCALE
        new_top = jnp.maximum(top, jnp.broadcast_to(tile_top, top.shape))
        groups = [
            jnp.exp2(s[:, u * HD : (u + 1) * HD] * LOG2_SCALE - new_top)
            for u in range(length // HD)
        ]
        lane_sum = functools.reduce(jnp.add, groups)
        p = jnp.concatenate([group.astype(jnp.bfloat16) for group in groups], 1)
        mixed = jnp.dot(p, v_ref[tile], preferred_element_type=jnp.float32)
        rescale = jnp.exp2(top - new_top)
        out = out * rescale + mixed
        total = total * rescale + lane_sum
        top = new_top
    return out, top, total


def finished(out_ref, top_ref, total_ref):
    total = jnp.maximum(jnp.sum(total_ref[...], axis=1, keepdims=True), TINY)
    return out_ref[...] * (1.0 / total), top_ref[...] + jnp.log2(total)


def write_packed(state, outs):
    out, level = state
    out = out.astype(jnp.bfloat16)
    lane = lax.broadcasted_iota(jnp.int32, (ROWS, 128), 1)
    head = lane % HEADS_DEV
    piece = lane % (3 * HEADS_DEV) // HEADS_DEV
    for i, o_ref in enumerate(outs):
        levels = jnp.zeros((ROWS, 128), jnp.float32)
        for tick in range(2):
            mine = lane // (3 * HEADS_DEV) == tick
            for h in range(HEADS_DEV):
                at = ((i * 2 + tick) * HEADS_DEV + h) * ROWS
                column = tick * WIDTH_DEV + h * HD
                o_ref[:, column : column + HD] = out[at : at + ROWS]
                levels = jnp.where(jnp.logical_and(mine, head == h), level[at : at + ROWS], levels)
        high = levels.astype(jnp.bfloat16).astype(jnp.float32)
        middle = (levels - high).astype(jnp.bfloat16).astype(jnp.float32)
        low = levels - high - middle
        pieces = jnp.where(piece == 0, high, jnp.where(piece == 1, middle, low))
        o_ref[:, 2 * WIDTH_DEV :] = pieces.astype(jnp.bfloat16)


def attend_rows(first_d, n_d, shift, lengths_ref, q_ref, k_ref, v_ref, state, started=True):
    cx = lax.axis_index("cx")
    cy = lax.axis_index("cy")
    base = cx * NY * ROWS - ((cx + shift) % NX * NY + cy) * KEYS
    least = [segment_start(lengths_ref, segment_of(tick)) + base for tick in range(2)]
    full = jnp.minimum(least[0], least[1]) >= KEYS - 1
    none = jnp.maximum(least[0], least[1]) + NY * ROWS - 1 < 0

    def run(masked):
        q = jnp.concatenate(
            [
                q_ref[cy ^ (first_d + i), tick, :, h * HD : (h + 1) * HD]
                for i in range(n_d)
                for tick in range(2)
                for h in range(HEADS_DEV)
            ],
            0,
        )
        last_offset = None
        if masked:
            row_id = lax.broadcasted_iota(jnp.int32, (n_d * BLOCK, 1), 0)
            owner = (first_d + row_id // BLOCK) ^ cy
            second = row_id // (BLOCK // 2) % 2 == 1
            last_offset = jnp.where(second, least[1], least[0]) + owner * ROWS + row_id % ROWS
        if started:
            held = tuple(ref[...] for ref in state)
        else:
            held = tuple(jnp.full((n_d * BLOCK, HD), x, jnp.float32) for x in EMPTY)
        length = KEYS if started else OWN_TILE
        result = update(held, q, k_ref, v_ref, last_offset, length)
        for ref, value in zip(state, result, strict=True):
            ref[...] = value

    @pl.when(full)
    def _():
        run(False)

    @pl.when(jnp.logical_not(jnp.logical_or(full, none)))
    def _():
        run(True)

    if not started:

        @pl.when(none)
        def _():
            for ref, value in zip(state, EMPTY, strict=True):
                ref[...] = jnp.full(ref.shape, value, jnp.float32)


def first_kernel(lengths_ref, q_ref, k_ref, v_ref, out_ref, top_ref, total_ref):
    def one(half, _):
        state = [ref.at[half] for ref in (out_ref, top_ref, total_ref)]
        attend_rows(2 * half, 2, 0, lengths_ref, q_ref, k_ref, v_ref, state, started=False)

    lax.fori_loop(0, 2, one, None)


def second_kernel(lengths_ref, q_ref, k_ref, v_ref, *refs):
    inputs, outs = refs[:3], refs[3:]

    def one(half, _):
        for source, target in zip(inputs, outs, strict=True):
            target[half] = source[half]
        state = [ref.at[half] for ref in outs]
        attend_rows(2 * half, 2, NX - 1, lengths_ref, q_ref, k_ref, v_ref, state)

    lax.fori_loop(0, 2, one, None)


def above_kernel(lengths_ref, q_ref, k_ref, v_ref, *refs):
    inputs, outs = refs[:3], refs[3:]
    for source, target in zip(inputs, outs, strict=True):
        target[...] = source[1]
    attend_rows(2, 2, 1, lengths_ref, q_ref, k_ref, v_ref, outs)


def far_kernel(lengths_ref, q_ref, k_ref, v_ref, *refs):
    inputs, outs, state = refs[:3], refs[3:5], refs[5:]
    for source, target in zip(inputs, state, strict=True):
        target[...] = source[...]
    attend_rows(2, 2, 2, lengths_ref, q_ref, k_ref, v_ref, state)
    write_packed(finished(*state), outs)


def near_kernel(d, *refs):
    lengths_ref, q_ref, k_above, v_above, k_far, v_far = refs[:6]
    inputs, o_ref, state = refs[6:9], refs[9], refs[10:]
    for source, target in zip(inputs, state, strict=True):
        target[...] = source[0, d * BLOCK : (d + 1) * BLOCK]
    attend_rows(d, 1, 1, lengths_ref, q_ref, k_above, v_above, state)
    attend_rows(d, 1, 2, lengths_ref, q_ref, k_far, v_far, state)
    write_packed(finished(*state), [o_ref])


def in_vmem(x):
    return pltpu.with_memory_space_constraint(x, pltpu.VMEM)


def in_hbm(x):
    return pltpu.with_memory_space_constraint(x, pltpu.HBM)


def attend(kernel, name, out_shape, scratch_rows, lengths, *operands):
    return pl.pallas_call(
        kernel,
        in_specs=[SMEM] + [VMEM] * len(operands),
        out_specs=[VMEM] * len(out_shape),
        out_shape=out_shape,
        scratch_shapes=[pltpu.VMEM((scratch_rows, HD), jnp.float32)] * 3 if scratch_rows else [],
        compiler_params=LARGE,
        name=name,
    )(lengths, *[in_vmem(x) for x in operands])


def merged(parts, tick, live):
    levels = []
    for part_ref in parts:
        pieces = part_ref[:, 2 * WIDTH_DEV :].astype(jnp.float32)
        levels.append(
            pieces
            + pltpu.roll(pieces, 128 - HEADS_DEV, 1)
            + pltpu.roll(pieces, 128 - 2 * HEADS_DEV, 1)
        )
    top = functools.reduce(jnp.maximum, levels)
    shares = [jnp.exp2(level - top) for level in levels]
    inverse = 1.0 / functools.reduce(jnp.add, shares)
    shares = [share * inverse for share in shares]
    columns = []
    for h in range(HEADS_DEV):
        total = jnp.zeros((ROWS, HD), jnp.float32)
        column = tick * WIDTH_DEV + h * HD
        lane = tick * 3 * HEADS_DEV + h
        for part_ref, share in zip(parts, shares, strict=True):
            part = part_ref[:, column : column + HD].astype(jnp.float32)
            total = total + share[:, lane : lane + 1] * part
        columns.append(total)
    return jnp.where(live, jnp.concatenate(columns, 1), 0.0)


def live_rows(lengths_ref, tick):
    first = (lax.axis_index("cx") * NY + lax.axis_index("cy")) * ROWS
    row = first + lax.broadcasted_iota(jnp.int32, (ROWS, 1), 0)
    return row < lengths_ref[segment_of(tick)]


def merge_one_kernel(lengths_ref, rows_ref, *refs):
    parts, (residual_ref, sum_ref) = refs[:NY], refs[NY:]
    total = rows_ref[...].astype(jnp.float32) + merged(parts, 0, live_rows(lengths_ref, 0))
    sum_ref[...] = total
    residual_ref[...] = total.astype(jnp.bfloat16)


def merge_two_kernel(lengths_ref, *refs):
    parts, attended_ref = refs[:NY], refs[NY]
    attended_ref[...] = merged(parts, 1, live_rows(lengths_ref, 1))


def add_kernel(attended_ref, passed_ref, fresh_ref, sum_one_ref, sum_ref, squares_ref):
    first = lax.axis_index("section") == 0
    incoming = jnp.where(first, fresh_ref[...].astype(jnp.float32), passed_ref[...].astype(jnp.float32))
    total = incoming + attended_ref[...]
    sum_ref[...] = total
    ones = jnp.ones((8, WIDTH_DEV), jnp.float32)
    for tick, rows in enumerate((sum_one_ref[...], total)):
        squares = lax.dot_general(
            ones,
            rows * rows,
            (((1,), (1,)), ((), ())),
            precision=lax.Precision.HIGHEST,
            preferred_element_type=jnp.float32,
        )
        squares_ref[tick : tick + 1, :] = squares[:1]


def norm_kernel(squares_ref, sum_one_ref, sum_two_ref, gain_ref, residual_ref, normed_ref):
    gain = gain_ref[...].astype(jnp.float32)
    row = lax.broadcasted_iota(jnp.int32, (ROWS, ROWS), 0)
    lane = lax.broadcasted_iota(jnp.int32, (ROWS, ROWS), 1)
    for tick, sum_ref in enumerate((sum_one_ref, sum_two_ref)):
        squares = functools.reduce(
            jnp.add, [squares_ref[i, tick : tick + 1, :] for i in range(squares_ref.shape[0])]
        )
        scale = lax.rsqrt(squares / FULL_WIDTH + EPSILON)
        column = jnp.sum(jnp.where(row == lane, scale, 0.0), axis=1, keepdims=True)
        residual_ref[tick] = sum_ref[...].astype(jnp.bfloat16)
        normed_ref[tick] = (sum_ref[...] * column * gain).astype(jnp.bfloat16)


def body(queries, key_rows, value_rows, section_rows, fresh_rows, norm_gain, segment_lengths):
    def along_x(value, by):
        return lax.ppermute(value, "cx", [(i, (i + by) % NX) for i in range(NX)])

    def across_y(value, d):
        return lax.ppermute(value, "cy", [(i, i ^ d) for i in range(NY)])

    k, v = key_rows[0], value_rows[0]
    k_below = along_x(k, 1)
    v_above = along_x(v, -1)
    q_own = jnp.broadcast_to(queries[:, 0], (NY, 2, ROWS, WIDTH_DEV))
    q_all = lax.all_to_all(q_own, "cy", 0, 0)
    v_next, k_below = lax.optimization_barrier((v, k_below))
    v_below = along_x(v_next, 1)
    k_above = along_x(k, -1)
    k_far = along_x(k_below, 1)

    both = [pltpu.VMEM((2, HALF, HD), jnp.float32)] * 3
    one = [pltpu.VMEM((HALF, HD), jnp.float32)] * 3
    packed = pltpu.VMEM((ROWS, PACKED), jnp.bfloat16)
    common = (segment_lengths, q_all)
    state = attend(first_kernel, "attend_own", both, 0, *common, k, v)
    v_next, state = lax.optimization_barrier((v_above, state))
    v_far = along_x(v_next, -1)
    state = attend(second_kernel, "attend_below", both, 0, *common, k_below, v_below, *state)
    upper = attend(above_kernel, "attend_above", one, 0, *common, k_above, v_above, *state)
    part_two, part_three = attend(
        far_kernel, "attend_far", [packed] * 2, HALF, *common, k_far, v_far, *upper
    )
    part_three = across_y(part_three, 3)
    part_two = across_y(part_two, 2)
    near = [
        attend(
            functools.partial(near_kernel, d),
            f"attend_near_{d}",
            [packed],
            BLOCK,
            *common,
            k_above,
            v_above,
            k_far,
            v_far,
            *state,
        )[0]
        for d in range(2)
    ]
    parts = (near[0], across_y(near[1], 1), part_two, part_three)

    rows_bf16 = pltpu.VMEM((ROWS, WIDTH_DEV), jnp.bfloat16)
    rows_f32 = pltpu.VMEM((ROWS, WIDTH_DEV), jnp.float32)
    parts = [in_vmem(part) for part in parts]
    residual_one, sum_one = pl.pallas_call(
        merge_one_kernel,
        in_specs=[SMEM] + [VMEM] * (1 + NY),
        out_specs=[VMEM] * 2,
        out_shape=[rows_bf16, rows_f32],
        compiler_params=SMALL,
        name="merge_one",
    )(segment_lengths, in_vmem(section_rows[0]), *parts)
    attended_two = pl.pallas_call(
        merge_two_kernel,
        in_specs=[SMEM] + [VMEM] * NY,
        out_specs=VMEM,
        out_shape=rows_f32,
        compiler_params=SMALL,
        name="merge_two",
    )(segment_lengths, *parts)
    count = lax.axis_size("section")
    passed = lax.ppermute(residual_one, "section", [(i, i + 1) for i in range(count - 1)])
    sum_two, squares = pl.pallas_call(
        add_kernel,
        in_specs=[VMEM] * 4,
        out_specs=[VMEM] * 2,
        out_shape=[rows_f32, pltpu.VMEM((2, ROWS), jnp.float32)],
        compiler_params=SMALL,
        name="add",
    )(*[in_vmem(x) for x in (attended_two, passed, fresh_rows, sum_one)])
    squares = lax.all_gather(squares, "tp")
    residual, normed = pl.pallas_call(
        norm_kernel,
        in_specs=[VMEM] * 4,
        out_specs=[VMEM] * 2,
        out_shape=[jax.ShapeDtypeStruct((2, ROWS, WIDTH_DEV), jnp.bfloat16)] * 2,
        compiler_params=SMALL,
        name="norm",
    )(in_vmem(squares), in_vmem(sum_one), in_vmem(sum_two), in_vmem(norm_gain))
    return residual[:, None], normed[:, None]


def solution(mesh):
    grid = Mesh(mesh.devices.reshape(8, NX, NY, 4), ("section", "cx", "cy", "tp"))
    cp = ("cx", "cy")
    in_specs = (
        P(None, "section", cp, "tp"),
        P("section", cp, "tp"),
        P("section", cp, "tp"),
        P("section", cp, "tp"),
        P(cp, "tp"),
        P("section", "tp"),
        P(),
    )
    out_specs = (P(None, "section", cp, "tp"), P(None, "section", cp, "tp"))
    return jax.shard_map(body, mesh=grid, in_specs=in_specs, out_specs=out_specs, check_vma=False)
```
